512 devices in a mesh: seq: 4 (over y), exp: 128 (over z, x, core).
Axes of the slice: x: 4, y: 4, z: 16, core: 2. Of those that a mesh axis runs over, the one named last changes fastest.
Arguments:
- out_grad: bfloat16 [65536, 4096], P(('seq', 'exp')), may hold values from -2 to 2
- expert_ids: int32 [65536, 2], P(('seq', 'exp')), may hold values from 0 to 127, all different within a row; in each aligned block of 128 rows (0 to 127, 128 to 255, ...) at most 3 rows name the same one
- route_weights: bfloat16 [65536, 2], P(('seq', 'exp')), may hold values from 0.099609375 to 1
- down_weight: bfloat16 [128, 768, 4096], P('exp', 'seq'), may hold values from -0.21875 to 0.21875
- gate_pre: bfloat16 [128, 1536, 768], P('exp', None, 'seq'), may hold values from -6 to 6
- up_pre: bfloat16 [128, 1536, 768], P('exp', None, 'seq'), may hold values from -6 to 6
Outputs:
- grad_gate: bfloat16 [128, 1536, 768], P('exp', None, 'seq')
- grad_up: bfloat16 [128, 1536, 768], P('exp', None, 'seq')
- route_grad: float32 [65536, 2], P(('seq', 'exp'))
The draws below stay inside these ranges and needn't reach their ends.
Inputs may be any that keep to these rules, and one draw needn't show every extreme that they name: `expert_ids`: A token's 2 slots name different experts. Among the slots of one device no expert is named more than 3 times, and in every draw some expert is named exactly 3 times by some device.
All inputs are finite; a program needn't handle non-finite values.
Results may differ from the reference program's by a relative error of at most 0.001.
Values may be sent and summed in bfloat16 or wider, within the bound.
A program may use at most 64 MiB of HBM per device.

```python
import math
import jax
import jax.numpy as jnp
import numpy as np
from jax import lax

D = 4096
FF = 768
TOP = 2
TOK_DEV = 128
EXPERTS = 128
CAP = 3
ROWS_E = 1536
TOKENS = 65536
N_SEQ = 4
N_EXP = 128


def block_levels(own_key, extent, pieces, smallest, high):
    loudness, own = 1.0, jax.random.fold_in(own_key, 6)
    for position, blocks in pieces:
        heights = jnp.exp(jax.random.uniform(jax.random.fold_in(own, position), (blocks,), jnp.float32, smallest / len(pieces), high / len(pieces)))
        loudness = loudness * jnp.repeat(heights, extent[position] // blocks).reshape([-1 if axis == position else 1 for axis in range(len(extent))])
    return loudness


def assign_block(stream_key, own, number, rows, count, top, bound, slope):
    ranking = jax.random.permutation(stream_key, count)
    packed, common = portions_of(count, rows * top, bound, slope, True), portions_of(count, rows * top, bound, slope, False)
    places = jnp.arange(count)

    def named(lengths, turn):
        used = int((lengths > 0).sum())
        fixed = max(1, used // 4)
        shifted = fixed + (places - fixed + turn * (used - fixed)) % max(1, count - fixed)
        return jnp.zeros((count,), jnp.int32).at[ranking[jnp.where(places < fixed, places, shifted)]].set(jnp.asarray(lengths, jnp.int32))

    lengths = jnp.where(number % 4 == 0, named(packed, number // 4), named(common, number - number // 4 - 1))
    mixed = jax.random.permutation(jax.random.fold_in(own, 3), count)
    source_of, taker = mixed[0:count // 2 * 2:2], mixed[1:count // 2 * 2:2]
    room = jnp.minimum(lengths[source_of] - 1, bound - lengths[taker]) // 2
    room = jnp.where((source_of == ranking[0]) | (taker == ranking[0]) | (lengths[taker] == 0), 0, jnp.maximum(room, 0))
    shifted = jax.random.randint(jax.random.fold_in(own, 4), (count // 2,), 0, 1 << 20) % (room + 1)
    lengths = lengths.at[source_of].add(-shifted).at[taker].add(shifted)
    items = jnp.searchsorted(jnp.cumsum(lengths), jnp.arange(rows * top), side="right").astype(jnp.int32)
    listing = items.reshape(top, rows).T
    listing = listing[jax.random.permutation(jax.random.fold_in(own, 1), rows)]
    turn = jax.random.randint(jax.random.fold_in(own, 2), (rows, 1), 0, top)
    return jnp.take_along_axis(listing, (jnp.arange(top)[None, :] + turn) % top, axis=1)


def portions_of(amount, total, reach, skew, full):
    loads = [(1 << 20) // math.isqrt(rank ** skew) + 1 for rank in range(1, amount + 1)]
    largest = reach if full else min(reach, max(-(-total // amount), total * loads[0] // sum(loads)))
    least = 1 if total - largest >= amount - 1 else 0
    counts, spare = [largest] + [least] * (amount - 1), total - largest - least * (amount - 1)
    while spare > 0:
        free = [i for i in range(1, amount) if counts[i] < largest] or [i for i in range(1, amount) if counts[i] < reach]
        mass, budget = sum([loads[i] for i in free]), spare
        for i in free:
            addition = min(reach - counts[i], max(1, budget * loads[i] // mass), spare)
            counts[i] = counts[i] + addition
            spare = spare - addition
    return np.array(counts)


def bell_draw(own_key, dims, spread, bound, pieces=(), held_as=jnp.bfloat16):
    result = spread * jax.random.normal(own_key, dims, jnp.float32)
    if pieces:
        result = result * block_levels(own_key, dims, pieces, -0.22, 0.18)
    return jnp.clip(result, -bound, bound).astype(held_as)


def setup_inputs(seed: int = 0) -> dict:
    splits = jax.random.split(jax.random.key(seed), 7)
    out_grad = bell_draw(splits[0], (TOKENS, D), 0.25, 2.0, ((0, 512),))
    expert_ids_keys = jax.random.split(jax.random.fold_in(splits[1], 1), TOKENS // TOK_DEV)
    expert_ids_turns = jax.random.permutation(jax.random.fold_in(splits[1], 3), TOKENS // TOK_DEV)
    expert_ids = jax.vmap(lambda own, number: assign_block(jax.random.fold_in(splits[1], 2), own, number, TOK_DEV, EXPERTS, TOP, CAP, 2))(expert_ids_keys, expert_ids_turns).reshape((TOKENS, TOP))
    route_weights = jnp.clip(jnp.exp(math.log(1.0) - 2.306499 * jax.random.uniform(splits[2], (TOKENS, TOP), jnp.float32) ** block_levels(splits[2], (TOKENS, TOP), ((0, 512),), -0.2, 0.2)), 0.099609375, 1.0).astype(jnp.bfloat16)
    down_weight = bell_draw(splits[3], (EXPERTS, FF, D), FF ** -0.5, 0.21875, ((0, 128), (1, 4)))
    gate_pre = bell_draw(splits[4], (EXPERTS, ROWS_E, FF), 1.5, 6.0, ((0, 128), (2, 4)))
    up_pre = bell_draw(splits[5], (EXPERTS, ROWS_E, FF), 1.0, 6.0, ((0, 128), (2, 4)))
    return {"out_grad": out_grad, "expert_ids": expert_ids, "route_weights": route_weights, "down_weight": down_weight, "gate_pre": gate_pre, "up_pre": up_pre}


def expert_backward(slot_rows, slot_weights, down_rows, gate_saved, up_saved):
    projected = lax.dot_general(slot_rows, down_rows, (((1,), (1,)), ((), ())), preferred_element_type=jnp.float32)
    gate_value = gate_saved.astype(jnp.float32)
    up_value = up_saved.astype(jnp.float32)
    sigmoid_gate = jax.nn.sigmoid(gate_value)
    activated = gate_value * sigmoid_gate
    partial_value = jnp.sum(activated * up_value * projected, axis=1)
    scaled = slot_weights.astype(jnp.float32)[:, None] * projected
    grad_up = scaled * activated
    grad_gate = scaled * up_value * sigmoid_gate * (1.0 + gate_value * (1.0 - sigmoid_gate))
    return grad_gate, grad_up, partial_value


def slot_positions(expert_ids):
    grouped = expert_ids.reshape(N_SEQ * N_EXP, TOK_DEV * TOP)

    def device_ranks(choices):
        onehot = (choices[:, None] == jnp.arange(EXPERTS, dtype=jnp.int32)[None, :]).astype(jnp.int32)
        return jnp.sum((jnp.cumsum(onehot, axis=0) - onehot) * onehot, axis=1)

    ranks = lax.map(device_ranks, grouped)
    sources = jnp.arange(N_SEQ * N_EXP, dtype=jnp.int32)[:, None]
    return (grouped * ROWS_E + sources * CAP + ranks).reshape(-1).astype(jnp.int32)


def reference(out_grad, expert_ids, route_weights, down_weight, gate_pre, up_pre):
    positions = slot_positions(expert_ids)
    sentinel = TOKENS * TOP
    slot_table = jnp.full((EXPERTS * ROWS_E,), sentinel, jnp.int32)
    slot_table = slot_table.at[positions].set(jnp.arange(sentinel, dtype=jnp.int32)).reshape(EXPERTS, ROWS_E)
    padded_rows = jnp.concatenate([out_grad, jnp.zeros((1, D), out_grad.dtype)], axis=0)
    padded_weights = jnp.concatenate([route_weights.reshape(-1), jnp.zeros((1,), route_weights.dtype)])

    def per_expert(inputs):
        entries, down_rows, gate_saved, up_saved = inputs
        slot_rows = padded_rows[entries // TOP]
        slot_weights = padded_weights[entries]
        grad_gate, grad_up, partial_value = expert_backward(slot_rows, slot_weights, down_rows, gate_saved, up_saved)
        return grad_gate.astype(jnp.bfloat16), grad_up.astype(jnp.bfloat16), partial_value

    grad_gate, grad_up, scores = lax.map(per_expert, (slot_table, down_weight, gate_pre, up_pre))
    route_grad = scores.reshape(-1)[positions].reshape(TOKENS, TOP)
    return grad_gate, grad_up, route_grad
```

```python
import jax
import jax.numpy as jnp
from jax import lax
from jax.sharding import PartitionSpec as P


def expert_backward(projected, slot_weights, gate_saved, up_saved):
    gate_value = gate_saved.astype(jnp.float32)
    up_value = up_saved.astype(jnp.float32)
    sigmoid_gate = jax.nn.sigmoid(gate_value)
    activated = gate_value * sigmoid_gate
    partial_value = jnp.sum(activated * up_value * projected, axis=1)
    scaled = slot_weights.astype(jnp.float32)[:, None] * projected
    grad_up = scaled * activated
    grad_gate = scaled * up_value * sigmoid_gate * (1.0 + gate_value * (1.0 - sigmoid_gate))
    return (grad_gate, grad_up, partial_value)


def per_device(out_grad, expert_ids, route_weights, down_weight, gate_pre, up_pre):
    tokens, slot_count = expert_ids.shape
    model_width = out_grad.shape[1]
    experts = lax.axis_size("exp")
    groups = lax.axis_size("seq")
    capacity = gate_pre.shape[1] // (groups * experts)
    flat_ids = expert_ids.reshape(-1)
    onehot = (flat_ids[:, None] == jnp.arange(experts, dtype=jnp.int32)[None, :]).astype(jnp.int32)
    slot_ranks = jnp.sum((jnp.cumsum(onehot, axis=0) - onehot) * onehot, axis=1)
    target = flat_ids * capacity + slot_ranks
    sentinel = tokens * slot_count
    slot_table = jnp.full((experts * capacity,), sentinel, jnp.int32)
    slot_table = slot_table.at[target].set(jnp.arange(sentinel, dtype=jnp.int32))
    padded_rows = jnp.concatenate([out_grad, jnp.zeros((1, model_width), out_grad.dtype)], axis=0)
    padded_weights = jnp.concatenate(
        [route_weights.reshape(-1), jnp.zeros((1,), route_weights.dtype)]
    )
    width = model_width // 128
    outgoing = padded_rows.reshape(tokens + 1, width, 128)[slot_table // slot_count]
    outgoing = outgoing.reshape(experts, capacity * width, 128)
    outgoing_weights = padded_weights[slot_table].reshape(experts, capacity)
    weight_rows = lax.all_gather(down_weight[0], "seq", axis=0, tiled=True)
    arrived, arrived_weights = (
        lax.all_to_all(outgoing, "exp", split_axis=0, concat_axis=0, tiled=True),
        lax.all_to_all(outgoing_weights, "exp", split_axis=0, concat_axis=0, tiled=True),
    )
    local_rows = arrived.reshape(experts * capacity, model_width)
    local_weights = arrived_weights.reshape(-1)
    all_weights = lax.all_gather(local_weights, "seq", axis=0, tiled=True)
    projected = lax.dot_general(
        weight_rows, local_rows, (((1,), (1,)), ((), ())), preferred_element_type=jnp.float32
    )
    projected = lax.all_to_all(projected, "seq", split_axis=0, concat_axis=1, tiled=True).T
    grad_gate, grad_up, partial_value = expert_backward(
        projected, all_weights, gate_pre[0], up_pre[0]
    )
    scores = lax.psum_scatter(partial_value, "seq", scatter_dimension=0, tiled=True)
    gate_out = grad_gate.astype(jnp.bfloat16)[None]
    up_out = grad_up.astype(jnp.bfloat16)[None]
    returned = lax.all_to_all(
        scores.reshape(experts, capacity), "exp", split_axis=0, concat_axis=0, tiled=True
    )
    route_grad = returned.reshape(-1)[target].reshape(tokens, slot_count)
    return (gate_out, up_out, route_grad)


def solution(mesh):
    placed = (
        P(("seq", "exp"), None),
        P(("seq", "exp"), None),
        P(("seq", "exp"), None),
        P("exp", "seq", None),
        P("exp", None, "seq"),
        P("exp", None, "seq"),
    )
    return jax.shard_map(
        per_device,
        mesh=mesh,
        in_specs=placed,
        out_specs=(P("exp", None, "seq"), P("exp", None, "seq"), P(("seq", "exp"), None)),
        check_vma=False,
    )
```

```python
import functools

import jax
import jax.numpy as jnp
from jax import lax
from jax.experimental import pallas as pl
from jax.experimental.pallas import tpu as pltpu
from jax.sharding import PartitionSpec as P

MESH = pl.DeviceIdType.MESH
WINDOW = 4
SEQ, ZN, PLANE = 4, 16, 8
SELF = 12
EXT = 128
F32, BF16 = jnp.float32, jnp.bfloat16
FAR = (4, 3, 5, 2, 6, 1, 7)
ALL_THIRD = (4, 3, 5, 2, 6, 1, 7, 0, 8, 9, 15, 10, 14, 11, 13)


def iota(shape, dim):
    return lax.broadcasted_iota(jnp.int32, shape, dim)


def hot(cond):
    return jnp.where(cond, 1.0, 0.0).astype(BF16)


def mm(a, b):
    return jnp.dot(a, b, preferred_element_type=F32)


def mm_t(a, b):
    return lax.dot_general(a, b, (((1,), (1,)), ((), ())), preferred_element_type=F32)


def kernel(
    x_ref, ids_ref, rw_ref, w_ref, g_ref, u_ref,
    gg_ref, gu_ref, rg_ref,
    s_main, r_main, s_third, r_third, t_main, x_main, t_third, x_third,
    w_all, g_all, u_all, g_perm, u_perm, acc, grads, back,
    score, score_in, total, total_in,
    z_s, z_r, zt_s, zt_r, p_s, p_r, y_s, y_r, b_s, b_r, ps_s, ps_r, zs_s, zs_r, local_sem,
):
    width = x_ref.shape[1]
    ff = w_ref.shape[0]
    block = g_ref.shape[1] // SEQ
    wide = width + EXT
    half = width // 2
    step = width // 4
    pieces = [(0, EXT + step)] + [(EXT + step * n, step) for n in range(1, 4)]

    s = lax.axis_index("seq")
    e = lax.axis_index("exp")
    z, x, c = e >> 3, (e >> 1) & 3, e & 1

    def z_to(k):
        return (s, (((z - 4 - k) & 15) << 3) | (e & 7))

    def z_from(k):
        return (s, (((z + 4 + k) & 15) << 3) | (e & 7))

    def p_to(j):
        return (s, (z << 3) | (((x + (j >> 1)) & 3) << 1) | ((c + (j & 1)) & 1))

    def p_from(j):
        return (s, (z << 3) | (((x - (j >> 1)) & 3) << 1) | ((c + (j & 1)) & 1))

    def y_to(q):
        return ((s + q) & 3, e)

    def y_from(q):
        return ((s - q) & 3, e)

    def remote(src, dst, send, recv, device):
        return pltpu.make_async_remote_copy(
            src_ref=src, dst_ref=dst, send_sem=send, recv_sem=recv,
            device_id=device, device_id_type=MESH,
        )

    barrier = pltpu.get_barrier_semaphore()
    for k in range(ZN):
        if k != SELF:
            pl.semaphore_signal(barrier, inc=1, device_id=z_from(k), device_id_type=MESH)
    for j in range(1, PLANE):
        pl.semaphore_signal(barrier, inc=1, device_id=p_from(j), device_id_type=MESH)
    for q in range(1, SEQ):
        pl.semaphore_signal(barrier, inc=1, device_id=y_from(q), device_id_type=MESH)

    own_w = pltpu.make_async_copy(w_ref, w_all.at[pl.ds(0, ff)], local_sem)
    own_w.start()

    ids0, ids1 = ids_ref[0:1, :], ids_ref[1:2, :]
    w0, w1 = rw_ref[0:1, :], rw_ref[1:2, :]
    tokens = ids_ref.shape[1]
    earlier = hot(iota((tokens, tokens), 0) < iota((tokens, tokens), 1))
    row = iota((256, tokens), 0)
    lane = iota((256, tokens), 1)
    expert = (((z - 4 - (row >> 4)) & 15) << 3) | (row & 7)
    upper = (row >> 3) & 1
    named0 = ids0 == expert
    named = named0 | (ids1 == expert)
    rank = mm(hot(named), earlier)
    is_main = named & (rank == upper.astype(F32))
    is_third = named & (rank == 2.0)
    m_main = hot(is_main)
    m_low, m_high = hot(is_third & (upper == 0)), hot(is_third & (upper == 1))
    value = jnp.where(named0, w0, w1)
    v_main = jnp.sum(jnp.where(is_main, value, 0.0), axis=1, keepdims=True)
    v_third = jnp.sum(jnp.where(is_third, value, 0.0), axis=1, keepdims=True)
    s_main[:, 0:EXT] = jnp.where(
        lane == 0, v_main, jnp.where(lane == 1, v_third, 0.0)
    ).astype(BF16)

    score[...] = jnp.zeros((8, 128), F32)
    own_w.wait()
    pl.semaphore_wait(barrier, ZN - 1 + PLANE - 1 + SEQ - 1)

    y_copies = []
    for q in range(1, SEQ):
        rows = pl.ds(ff * q, ff)
        lanes = pl.ds(pl.multiple_of(((s + q) & 3) * block, 128), block)
        y_copies.append([
            remote(g_ref.at[:, lanes], g_all.at[rows], y_s.at[0, q], y_r.at[0, q], y_to(q)),
            remote(u_ref.at[:, lanes], u_all.at[rows], y_s.at[1, q], y_r.at[1, q], y_to(q)),
            remote(w_all.at[pl.ds(0, ff)], w_all.at[rows], y_s.at[2, q], y_r.at[2, q], y_to(q)),
        ])

    pending = []

    def issue(copy):
        if len(pending) >= WINDOW:
            pending.pop(0).wait_send()
        copy.start()
        pending.append(copy)

    def main_copy(k, start, size, n):
        part = (pl.ds(16 * k, 16), pl.ds(start, size))
        return remote(s_main.at[part], r_main.at[part], z_s.at[k, n], z_r.at[k, n], z_to(k))

    whole = {k: main_copy(k, 0, wide, 0) for k in (8, 9, 15, 10, 14, 11, 13, 0)}
    part = {
        (k, n): main_copy(k, start, size, n) for n, (start, size) in enumerate(pieces) for k in FAR
    }
    third = {
        k: remote(
            s_third.at[pl.ds(16 * k, 16)], r_third.at[pl.ds(16 * k, 16)],
            zt_s.at[k], zt_r.at[k], z_to(k),
        )
        for k in ALL_THIRD
    }

    for start in range(0, width, 1024):
        s_main[128:256, EXT + start : EXT + start + 1024] = mm(
            m_main[128:256], x_ref[:, start : start + 1024]
        ).astype(BF16)
    for k in (8, 9, 15, 10):
        issue(whole[k])
    for n in (0, 1, 2):
        for q in range(1, SEQ):
            y_copies[q - 1][n].start()
    for start in range(0, width, 1024):
        s_main[0:128, EXT + start : EXT + start + 1024] = mm(
            m_main[0:128], x_ref[:, start : start + 1024]
        ).astype(BF16)
    for start in range(0, half, 1024):
        s_third[:, start : start + 1024] = (
            mm(m_low, x_ref[:, start : start + 1024])
            + mm(m_high, x_ref[:, half + start : half + start + 1024])
        ).astype(BF16)
    for k in (14, 0, 11, 13):
        issue(whole[k])
    r_main[16 * SELF : 16 * SELF + 16, :] = s_main[16 * SELF : 16 * SELF + 16, :]
    r_third[16 * SELF : 16 * SELF + 16, :] = s_third[16 * SELF : 16 * SELF + 16, :]

    out_row = iota((128, 128), 0)
    j_of = out_row >> 4
    p_of = (((x + (j_of >> 1)) & 3) << 1) | ((c + (j_of & 1)) & 1)
    regroup = hot(
        iota((128, 128), 1) == ((out_row >> 1) & 7) * 16 + (out_row & 1) * 8 + p_of
    )
    out_row = iota((128, 256), 0)
    j_of = out_row >> 4
    p_of = (((x + (j_of >> 1)) & 3) << 1) | ((c + (j_of & 1)) & 1)
    low_row = (out_row & 15) * 16 + p_of
    regroup_low = hot(iota((128, 256), 1) == low_row)
    regroup_high = hot(iota((128, 256), 1) == low_row + 8)

    plane_copies = []

    def plane_send(src, dst, start, size, n):
        group = []
        for j in range(1, PLANE):
            area = (pl.ds(16 * j, 16), pl.ds(start, size))
            copy = remote(src.at[area], dst.at[area], p_s.at[n, j], p_r.at[n, j], p_to(j))
            copy.start()
            group.append(copy)
        plane_copies.extend(group)
        dst[0:16, start : start + size] = src[0:16, start : start + size]
        return group

    def split(start, size):
        at = start
        while at < start + size:
            span = min(1152, start + size - at)
            yield at, span
            at += span

    def main_forward(h, start, size, n):
        base = 128 if h == 0 else 0
        for at, span in split(start, size):
            t_main[h, :, at : at + span] = mm(
                regroup, r_main[base : base + 128, at : at + span]
            ).astype(BF16)
        return plane_send(t_main.at[h], x_main.at[h], start, size, n)

    def third_forward(n):
        for at, span in split(0, half):
            rows = r_third[:, at : at + span]
            t_third[:, at : at + span] = mm(regroup_low, rows).astype(BF16)
            t_third[:, half + at : half + at + span] = mm(regroup_high, rows).astype(BF16)
        return plane_send(t_third, x_third, 0, width, n)

    def natural(index):
        chunk, low = index >> 7, index & 127
        j = low >> 4
        is3 = chunk == 1
        k = jnp.where(is3, low & 15, ((low >> 1) & 7) + jnp.where(chunk == 0, 8, 0))
        r = jnp.where(is3, 2, low & 1)
        source = (((x - (j >> 1)) & 3) << 1) | ((c + (j & 1)) & 1)
        return ((z + 4 + k) & 15) * 24 + source * 3 + r

    def gates_ready():
        own = pl.ds(pl.multiple_of(s * block, 128), block)
        g_all[0:ff, :] = g_ref[:, own]
        u_all[0:ff, :] = u_ref[:, own]
        order = hot(iota((block, block), 0) == natural(iota((block, block), 1)))
        for q in range(SEQ):
            if q:
                y_copies[q - 1][0].wait_recv()
                y_copies[q - 1][1].wait_recv()
            rows = slice(ff * q, ff * q + ff)
            g_perm[rows, :] = mm(g_all[rows, :], order).astype(BF16)
            u_perm[rows, :] = mm(u_all[rows, :], order).astype(BF16)

    back_copies = []

    def finish(chunk, weights):
        lanes = slice(128 * chunk, 128 * chunk + 128)
        summed = jnp.zeros((1, 128), F32)
        for q in (2, 1, 3, 0):
            rows = slice(ff * q, ff * q + ff)
            projected = acc[rows, :]
            gate = g_perm[rows, lanes].astype(F32)
            up = u_perm[rows, lanes].astype(F32)
            sig = jax.nn.sigmoid(gate)
            activated = gate * sig
            summed = summed + jnp.sum(activated * up * projected, axis=0, keepdims=True)
            scaled = weights * projected
            grad_up = (scaled * activated).astype(BF16)
            grad_gate = (scaled * up * sig * (1.0 + gate * (1.0 - sig))).astype(BF16)
            if q:
                grads[chunk, rows, 0:128] = grad_gate
                grads[chunk, rows, 128:256] = grad_up
                copy = remote(
                    grads.at[chunk, pl.ds(ff * q, ff)], back.at[chunk, q],
                    b_s.at[chunk, q], b_r.at[chunk, q], y_from(q),
                )
                copy.start()
                back_copies.append(copy)
            else:
                back[chunk, 0, :, 0:128] = grad_gate
                back[chunk, 0, :, 128:256] = grad_up
        score[chunk : chunk + 1, :] = summed

    def slot_weights(h):
        pick = hot(iota((16, 128), 0) == iota((16, 128), 1))
        return mm_t(pick, x_main[h, :, 0:EXT])

    def spread(weights, h):
        src, dst = iota((128, 128), 0), iota((128, 128), 1)
        match = (src & 1 == 0) & (src >> 4 == dst >> 4)
        match = match & (dst & 15 == ((src >> 1) & 7) + (8 if h == 0 else 0))
        return mm(weights.astype(BF16), hot(match))

    for k in ALL_THIRD[:5]:
        issue(third[k])
    for k in (8, 9, 15, 10, 14, 11, 13):
        whole[k].wait_recv()
    near_group = main_forward(0, 0, wide, 0)
    for k in ALL_THIRD[5:9]:
        issue(third[k])
    gates_ready()
    for k in ALL_THIRD[9:]:
        issue(third[k])
    for k in FAR[:4]:
        issue(part[k, 0])
    for k in ALL_THIRD:
        third[k].wait_recv()
    third_group = third_forward(1)
    for k in FAR[4:]:
        issue(part[k, 0])
    for group in y_copies:
        group[2].wait_recv()
    for copy in near_group:
        copy.wait_recv()
    acc[...] = mm_t(w_all[...], x_main[0, :, EXT:])
    near_weights = slot_weights(0)
    finish(0, near_weights[0:1, :])
    far_groups = []

    def far_forward(n):
        if n == 0:
            whole[0].wait_recv()
        for k in FAR:
            part[k, n].wait_recv()
        far_groups.append(main_forward(1, pieces[n][0], pieces[n][1], 2 + n))

    def far_product(n):
        for copy in far_groups[n]:
            copy.wait_recv()
        product = mm_t(
            w_all[:, step * n : step * n + step],
            x_main[1, :, EXT + step * n : EXT + step * n + step],
        )
        if n == 0:
            acc[...] = product
        else:
            acc[...] += product

    for k in FAR[:4]:
        issue(part[k, 1])
    far_forward(0)
    for k in FAR[4:]:
        issue(part[k, 1])
    for copy in third_group:
        copy.wait_recv()
    acc[...] = mm_t(w_all[...], x_third[...])
    for copy in far_groups[0]:
        copy.wait_recv()
    far_weights = slot_weights(1)
    third_weights = spread(near_weights, 0) + spread(far_weights, 1)
    finish(1, third_weights[1:2, :])
    for k in FAR[:4]:
        issue(part[k, 2])
    far_forward(1)
    acc[...] = mm_t(w_all[:, 0:step], x_main[1, :, EXT : EXT + step])
    for k in FAR[4:]:
        issue(part[k, 2])
    for k in FAR[:4]:
        issue(part[k, 3])
    far_forward(2)
    far_product(1)
    for k in FAR[4:]:
        issue(part[k, 3])
    far_product(2)
    far_forward(3)
    far_product(3)
    finish(2, far_weights[0:1, :])

    score_copies = []
    for j in range(1, PLANE):
        copy = remote(score, score_in.at[j], ps_s.at[j], ps_r.at[j], p_from(j))
        copy.start()
        score_copies.append(copy)
    place = iota((8, 128), 1)
    gathered = jnp.where(place >> 4 == 0, score[...], 0.0)
    for j in range(1, PLANE):
        score_copies[j - 1].wait_recv()
        gathered = jnp.where(place >> 4 == j, score_in[j], gathered)
    total[...] = gathered
    total_copies = {}
    for k in FAR + (0, 8, 9, 15, 10, 14, 11, 13):
        copy = remote(total, total_in.at[k], zs_s.at[k], zs_r.at[k], z_from(k))
        copy.start()
        total_copies[k] = copy

    restore = hot(natural(iota((block, block), 0)) == iota((block, block), 1))
    for copy in back_copies:
        copy.wait_recv()
    for q in range(SEQ):
        lanes = pl.ds(pl.multiple_of(((s + q) & 3) * block, 128), block)
        for ref, first in ((gg_ref, 0), (gu_ref, 128)):
            value = jnp.concatenate([back[n, q, :, first : first + 128] for n in range(3)], axis=1)
            ref[:, lanes] = mm(value, restore).astype(BF16)

    is3 = iota((8, 128), 0) == 1
    low = (place >> 1) & 7
    is_near = iota((8, 128), 0) == 0
    slot = jnp.where(is3, place & 15, jnp.where(is_near, low + 8, low))
    found = jnp.where(slot == SELF, total[...], 0.0)
    for k in FAR + (0, 8, 9, 15, 10, 14, 11, 13):
        total_copies[k].wait_recv()
        found = jnp.where(slot == k, total_in[k], found)
    columns = jnp.transpose(jnp.concatenate([found, jnp.zeros((120, 128), F32)], axis=0))
    row = iota((128, 128), 0)
    j = row >> 4
    target = (((x + (j >> 1)) & 3) << 1) | ((c + (j & 1)) & 1)
    result0 = jnp.zeros((1, 128), F32)
    result1 = jnp.zeros((1, 128), F32)
    for chunk in range(3):
        if chunk == 1:
            k, r = row & 15, jnp.full((128, 128), 2, jnp.int32)
        else:
            k, r = ((row >> 1) & 7) + (8 if chunk == 0 else 0), row & 1
        expert = (((z - 4 - k) & 15) << 3) | target
        first, second = ids0 == expert, ids1 == expert
        match = mm(hot(first | second), earlier) == r.astype(F32)
        column = columns[:, chunk : chunk + 1]
        result0 += jnp.sum(jnp.where(first & match, column, 0.0), axis=0, keepdims=True)
        result1 += jnp.sum(jnp.where(second & match, column, 0.0), axis=0, keepdims=True)
    rg_ref[0:1, :] = result0
    rg_ref[1:2, :] = result1

    for copy in pending + plane_copies + back_copies + score_copies + list(total_copies.values()):
        copy.wait_send()
    for group in y_copies:
        for copy in group:
            copy.wait_send()


def per_device(out_grad, expert_ids, route_weights, down_weight, gate_pre, up_pre):
    tokens, width = out_grad.shape
    ff = down_weight.shape[1]
    rows = gate_pre.shape[1]
    block = rows // SEQ
    wide = width + EXT
    vmem = pl.BlockSpec(memory_space=pltpu.VMEM)
    dma = pltpu.SemaphoreType.DMA
    gate_out, up_out, route = pl.pallas_call(
        kernel,
        out_shape=(
            jax.ShapeDtypeStruct((ff, rows), BF16),
            jax.ShapeDtypeStruct((ff, rows), BF16),
            jax.ShapeDtypeStruct((2, tokens), F32),
        ),
        in_specs=[vmem, vmem, vmem, pl.BlockSpec(memory_space=pl.ANY), vmem, vmem],
        out_specs=(vmem, vmem, vmem),
        scratch_shapes=[
            pltpu.VMEM((256, wide), BF16),
            pltpu.VMEM((256, wide), BF16),
            pltpu.VMEM((256, width // 2), BF16),
            pltpu.VMEM((256, width // 2), BF16),
            pltpu.VMEM((2, 128, wide), BF16),
            pltpu.VMEM((2, 128, wide), BF16),
            pltpu.VMEM((128, width), BF16),
            pltpu.VMEM((128, width), BF16),
            pltpu.VMEM((SEQ * ff, width), BF16),
            pltpu.VMEM((SEQ * ff, block), BF16),
            pltpu.VMEM((SEQ * ff, block), BF16),
            pltpu.VMEM((SEQ * ff, block), BF16),
            pltpu.VMEM((SEQ * ff, block), BF16),
            pltpu.VMEM((SEQ * ff, 128), F32),
            pltpu.VMEM((3, SEQ * ff, 256), BF16),
            pltpu.VMEM((3, SEQ, ff, 256), BF16),
            pltpu.VMEM((8, 128), F32),
            pltpu.VMEM((PLANE, 8, 128), F32),
            pltpu.VMEM((8, 128), F32),
            pltpu.VMEM((ZN, 8, 128), F32),
            dma((ZN, 4)), dma((ZN, 4)), dma((ZN,)), dma((ZN,)),
            dma((6, PLANE)), dma((6, PLANE)), dma((3, SEQ)), dma((3, SEQ)),
            dma((3, SEQ)), dma((3, SEQ)), dma((PLANE,)), dma((PLANE,)),
            dma((ZN,)), dma((ZN,)), dma,
        ],
        compiler_params=pltpu.CompilerParams(
            collective_id=0, has_side_effects=True, vmem_limit_bytes=56 * 2**20
        ),
        cost_estimate=pl.CostEstimate(
            flops=2 * SEQ * ff * width * block, bytes_accessed=8 * 2**20, transcendentals=0
        ),
        name="expert_backward",
    )(
        out_grad,
        expert_ids.T,
        route_weights.T.astype(F32),
        down_weight[0],
        gate_pre[0].T,
        up_pre[0].T,
    )
    return gate_out.T[None], up_out.T[None], route.T


def solution(mesh):
    placed = (
        P(("seq", "exp"), None),
        P(("seq", "exp"), None),
        P(("seq", "exp"), None),
        P("exp", "seq", None),
        P("exp", None, "seq"),
        P("exp", None, "seq"),
    )
    return jax.shard_map(
        per_device,
        mesh=mesh,
        in_specs=placed,
        out_specs=(P("exp", None, "seq"), P("exp", None, "seq"), P(("seq", "exp"), None)),
        check_vma=False,
    )
```

```python
import functools

import jax
import jax.numpy as jnp
from jax import lax
from jax.experimental import pallas as pl
from jax.experimental.pallas import tpu as pltpu
from jax.sharding import PartitionSpec as P

MESH = pl.DeviceIdType.MESH
WINDOW = 8
PIECES = 4
SEQ, ZN, PLANE = 4, 16, 8
SELF = 12
EXT = 128
F32, BF16 = jnp.float32, jnp.bfloat16
FAR = (4, 3, 5, 2, 6, 1, 7)
ALL_THIRD = (4, 3, 5, 2, 6, 1, 7, 0, 8, 9, 15, 10, 14, 11, 13)


def iota(shape, dim):
    return lax.broadcasted_iota(jnp.int32, shape, dim)


def hot(cond):
    return jnp.where(cond, 1.0, 0.0).astype(BF16)


def mm(a, b):
    return jnp.dot(a, b, preferred_element_type=F32)


def mm_t(a, b):
    return lax.dot_general(a, b, (((1,), (1,)), ((), ())), preferred_element_type=F32)


def kernel(
    spare, x_ref, ids_ref, rw_ref, w_ref, g_ref, u_ref,
    gg_ref, gu_ref, rg_ref, over_ref,
    s_main, r_main, s_third, r_third, t_main, x_main, t_third, x_third,
    w_all, g_all, u_all, g_perm, u_perm, acc, grads, back,
    score, score_in, total, total_in, over, over_in,
    z_s, z_r, zt_s, zt_r, p_s, p_r, y_s, y_r, b_s, b_r, ps_s, ps_r, zs_s, zs_r, o_s, o_r, local_sem,
):
    width = x_ref.shape[1]
    ff = w_ref.shape[0]
    block = g_ref.shape[1] // SEQ
    wide = width + EXT
    parts = 16 // spare
    span3 = width // parts
    step = width // PIECES
    pieces = [(EXT + step * n, step) for n in range(PIECES)]

    s = lax.axis_index("seq")
    e = lax.axis_index("exp")
    z, x, c = e >> 3, (e >> 1) & 3, e & 1

    def z_to(k):
        return (s, (((z - 4 - k) & 15) << 3) | (e & 7))

    def z_from(k):
        return (s, (((z + 4 + k) & 15) << 3) | (e & 7))

    def p_to(j):
        return (s, (z << 3) | (((x + (j >> 1)) & 3) << 1) | ((c + (j & 1)) & 1))

    def p_from(j):
        return (s, (z << 3) | (((x - (j >> 1)) & 3) << 1) | ((c + (j & 1)) & 1))

    def y_to(q):
        return ((s + q) & 3, e)

    def y_from(q):
        return ((s - q) & 3, e)

    def remote(src, dst, send, recv, device):
        return pltpu.make_async_remote_copy(
            src_ref=src, dst_ref=dst, send_sem=send, recv_sem=recv,
            device_id=device, device_id_type=MESH,
        )

    barrier = pltpu.get_barrier_semaphore()
    for k in range(ZN):
        if k != SELF:
            pl.semaphore_signal(barrier, inc=1, device_id=z_from(k), device_id_type=MESH)
    for j in range(1, PLANE):
        pl.semaphore_signal(barrier, inc=1, device_id=p_from(j), device_id_type=MESH)
    for q in range(1, SEQ):
        pl.semaphore_signal(barrier, inc=1, device_id=y_from(q), device_id_type=MESH)

    own_w = pltpu.make_async_copy(w_ref, w_all.at[pl.ds(0, ff)], local_sem)
    own_w.start()

    ids0, ids1 = ids_ref[0:1, :], ids_ref[1:2, :]
    w0, w1 = rw_ref[0:1, :].astype(F32), rw_ref[1:2, :].astype(F32)
    tokens = ids_ref.shape[1]
    earlier = hot(iota((tokens, tokens), 0) < iota((tokens, tokens), 1))
    row = iota((256, tokens), 0)
    lane = iota((256, tokens), 1)
    expert = (((z - 4 - (row >> 4)) & 15) << 3) | (row & 7)
    upper = (row >> 3) & 1
    named0 = ids0 == expert
    named = named0 | (ids1 == expert)
    rank = mm(hot(named), earlier)
    is_main = named & (rank == upper.astype(F32))
    is_third = named & (rank == 2.0)
    m_main = hot(is_main)
    m_third = hot(is_third)
    have = mm_t(jnp.ones((16, tokens), BF16), m_third)
    src, dst = iota((256, 256), 0), iota((256, 256), 1)
    before = (src >> 4 == dst >> 4) & (src & 8 == 0)
    ahead = mm(have.astype(BF16), hot(before & (src & 7 < dst & 7)))
    held = mm(have.astype(BF16), hot(before))
    excess = jnp.max(jnp.where(held > spare, 1.0, 0.0))
    packed = (src >> 4 == dst >> 4) & (dst & 8 == 0)
    packed = packed & (ahead[0:1, :] == (src & (spare - 1)).astype(F32))
    m_packed = mm(hot(packed), m_third)
    part_of = (row & 15) >> (spare.bit_length() - 1)
    m_part = [hot((m_packed > 0.5) & (part_of == n)) for n in range(parts)]
    rank_in = mm(hot((src >> 4 == dst >> 4) & (dst & 8 == 0) & (dst & 7 < src & 7)), m_third)
    v_spot = jnp.sum(rank_in, axis=1, keepdims=True)
    v_have = jnp.sum(m_third.astype(F32), axis=1, keepdims=True)
    v_spot = jnp.where((v_have > 0.5) & (v_spot < spare - 0.5), v_spot + 1.0, 0.0)
    value = jnp.where(named0, w0, w1)
    v_main = jnp.sum(jnp.where(is_main, value, 0.0), axis=1, keepdims=True)
    v_third = jnp.sum(jnp.where(is_third, value, 0.0), axis=1, keepdims=True)
    s_main[:, 0:EXT] = jnp.where(
        lane == 0,
        v_main,
        jnp.where(lane == 1, v_third, jnp.where(lane == 2, v_spot, jnp.where(lane == 3, excess, 0.0))),
    ).astype(BF16)

    score[...] = jnp.zeros((8, 128), F32)
    own_w.wait()
    pl.semaphore_wait(barrier, ZN - 1 + PLANE - 1 + SEQ - 1)

    y_copies = []
    for q in range(1, SEQ):
        rows = pl.ds(ff * q, ff)
        lanes = pl.ds(pl.multiple_of(((s + q) & 3) * block, 128), block)
        y_copies.append([
            remote(g_ref.at[:, lanes], g_all.at[rows], y_s.at[0, q], y_r.at[0, q], y_to(q)),
            remote(u_ref.at[:, lanes], u_all.at[rows], y_s.at[1, q], y_r.at[1, q], y_to(q)),
            remote(w_all.at[pl.ds(0, ff)], w_all.at[rows], y_s.at[2, q], y_r.at[2, q], y_to(q)),
        ])

    pending = []

    def issue(copy):
        if len(pending) >= WINDOW:
            pending.pop(0).wait_send()
        copy.start()
        pending.append(copy)

    def main_copy(k, start, size, n):
        part = (pl.ds(16 * k, 16), pl.ds(start, size))
        return remote(s_main.at[part], r_main.at[part], z_s.at[k, n], z_r.at[k, n], z_to(k))

    whole = {k: main_copy(k, 0, wide, 0) for k in (8, 9, 15, 10, 14, 11, 13, 0)}
    part = {
        (k, n): main_copy(k, start, size, n) for n, (start, size) in enumerate(pieces) for k in FAR
    }
    extra = {k: main_copy(k, 0, EXT, PIECES) for k in FAR}
    third = {
        k: remote(
            s_third.at[pl.ds(16 * k, 16)], r_third.at[pl.ds(16 * k, 16)],
            zt_s.at[k], zt_r.at[k], z_to(k),
        )
        for k in ALL_THIRD
    }

    for start in range(0, width, 1024):
        s_main[128:256, EXT + start : EXT + start + 1024] = mm(
            m_main[128:256], x_ref[:, start : start + 1024]
        ).astype(BF16)
    for k in (8, 9, 15, 10):
        issue(whole[k])
    for n in (0, 1, 2):
        for q in range(1, SEQ):
            y_copies[q - 1][n].start()
    for start in range(0, width, 1024):
        s_main[0:128, EXT + start : EXT + start + 1024] = mm(
            m_main[0:128], x_ref[:, start : start + 1024]
        ).astype(BF16)
    packed_rows = mm(m_part[0], x_ref[:, 0:span3])
    for n in range(1, parts):
        packed_rows += mm(m_part[n], x_ref[:, span3 * n : span3 * n + span3])
    s_third[...] = packed_rows.astype(BF16)
    for k in (14, 0, 11, 13):
        issue(whole[k])
    r_main[16 * SELF : 16 * SELF + 16, :] = s_main[16 * SELF : 16 * SELF + 16, :]
    r_third[16 * SELF : 16 * SELF + 16, :] = s_third[16 * SELF : 16 * SELF + 16, :]

    out_row = iota((128, 128), 0)
    j_of = out_row >> 4
    p_of = (((x + (j_of >> 1)) & 3) << 1) | ((c + (j_of & 1)) & 1)
    regroup = hot(
        iota((128, 128), 1) == ((out_row >> 1) & 7) * 16 + (out_row & 1) * 8 + p_of
    )
    plane_copies = []

    def plane_send(src, dst, start, size, n):
        group = []
        for j in range(1, PLANE):
            area = (pl.ds(16 * j, 16), pl.ds(start, size))
            copy = remote(src.at[area], dst.at[area], p_s.at[n, j], p_r.at[n, j], p_to(j))
            copy.start()
            group.append(copy)
        plane_copies.extend(group)
        dst[0:16, start : start + size] = src[0:16, start : start + size]
        return group

    def split(start, size):
        at = start
        while at < start + size:
            span = min(1152, start + size - at)
            yield at, span
            at += span

    def main_forward(h, start, size, n):
        base = 128 if h == 0 else 0
        for at, span in split(start, size):
            t_main[h, :, at : at + span] = mm(
                regroup, r_main[base : base + 128, at : at + span]
            ).astype(BF16)
        return plane_send(t_main.at[h], x_main.at[h], start, size, n)

    def third_forward(n):
        out_row = iota((128, 256), 0)
        column = iota((128, 256), 1)
        j = out_row >> 4
        p = (((x + (j >> 1)) & 3) << 1) | ((c + (j & 1)) & 1)
        chosen = mm(hot(column == (out_row & 15) * 16 + p), r_main[:, 0:EXT])
        spot = chosen[:, 2:3] - 1.0
        spot = (out_row & 15 == column >> 4) & (spot == (column & (spare - 1)).astype(F32))
        part_of = (column & 15) >> (spare.bit_length() - 1)
        for m in range(parts):
            match = hot(spot & (part_of == m))
            t_third[:, span3 * m : span3 * m + span3] = mm(match, r_third[...]).astype(BF16)
        return plane_send(t_third, x_third, 0, width, n)

    def natural(index):
        chunk, low = index >> 7, index & 127
        j = low >> 4
        is3 = chunk == 1
        k = jnp.where(is3, low & 15, ((low >> 1) & 7) + jnp.where(chunk == 0, 8, 0))
        r = jnp.where(is3, 2, low & 1)
        source = (((x - (j >> 1)) & 3) << 1) | ((c + (j & 1)) & 1)
        return ((z + 4 + k) & 15) * 24 + source * 3 + r

    def gates_ready():
        own = pl.ds(pl.multiple_of(s * block, 128), block)
        g_all[0:ff, :] = g_ref[:, own]
        u_all[0:ff, :] = u_ref[:, own]
        order = hot(iota((block, block), 0) == natural(iota((block, block), 1)))
        for q in range(SEQ):
            if q:
                y_copies[q - 1][0].wait_recv()
                y_copies[q - 1][1].wait_recv()
            rows = slice(ff * q, ff * q + ff)
            g_perm[rows, :] = mm(g_all[rows, :], order).astype(BF16)
            u_perm[rows, :] = mm(u_all[rows, :], order).astype(BF16)

    back_copies = []

    def finish(chunk, weights):
        lanes = slice(128 * chunk, 128 * chunk + 128)
        summed = jnp.zeros((1, 128), F32)
        for q in (2, 1, 3, 0):
            rows = slice(ff * q, ff * q + ff)
            projected = acc[rows, :]
            gate = g_perm[rows, lanes].astype(F32)
            up = u_perm[rows, lanes].astype(F32)
            sig = jax.nn.sigmoid(gate)
            activated = gate * sig
            summed = summed + jnp.sum(activated * up * projected, axis=0, keepdims=True)
            scaled = weights * projected
            grad_up = (scaled * activated).astype(BF16)
            grad_gate = (scaled * up * sig * (1.0 + gate * (1.0 - sig))).astype(BF16)
            if q:
                grads[chunk, rows, 0:128] = grad_gate
                grads[chunk, rows, 128:256] = grad_up
                copy = remote(
                    grads.at[chunk, pl.ds(ff * q, ff)], back.at[chunk, q],
                    b_s.at[chunk, q], b_r.at[chunk, q], y_from(q),
                )
                copy.start()
                back_copies.append(copy)
            else:
                back[chunk, 0, :, 0:128] = grad_gate
                back[chunk, 0, :, 128:256] = grad_up
        score[chunk : chunk + 1, :] = summed

    def slot_weights(h):
        pick = hot(iota((16, 128), 0) == iota((16, 128), 1))
        return mm_t(pick, x_main[h, :, 0:EXT])

    def spread(weights, h):
        src, dst = iota((128, 128), 0), iota((128, 128), 1)
        match = (src & 1 == 0) & (src >> 4 == dst >> 4)
        match = match & (dst & 15 == ((src >> 1) & 7) + (8 if h == 0 else 0))
        return mm(weights.astype(BF16), hot(match))

    for k in ALL_THIRD[:7]:
        issue(extra[k])
        issue(third[k])
    for k in (8, 9, 15, 10, 14, 11, 13):
        whole[k].wait_recv()
    near_group = main_forward(0, 0, wide, 0)
    for k in ALL_THIRD[7:]:
        issue(third[k])
    gates_ready()
    for k in FAR:
        issue(part[k, 0])
    for k in FAR:
        extra[k].wait_recv()
    for k in ALL_THIRD:
        third[k].wait_recv()
    whole[0].wait_recv()
    third_group = third_forward(1)
    for k in FAR[:4]:
        issue(part[k, 1])
    for group in y_copies:
        group[2].wait_recv()
    for copy in near_group:
        copy.wait_recv()
    acc[...] = mm_t(w_all[...], x_main[0, :, EXT:])
    near_weights = slot_weights(0)
    finish(0, near_weights[0:1, :])
    far_groups = []

    def far_forward(n):
        for k in FAR:
            part[k, n].wait_recv()
        start, size = pieces[n]
        if n == 0:
            start, size = 0, EXT + size
        far_groups.append(main_forward(1, start, size, 2 + n))

    def far_product(n):
        for copy in far_groups[n]:
            copy.wait_recv()
        product = mm_t(
            w_all[:, step * n : step * n + step],
            x_main[1, :, EXT + step * n : EXT + step * n + step],
        )
        if n == 0:
            acc[...] = product
        else:
            acc[...] += product

    far_forward(0)
    for k in FAR[4:]:
        issue(part[k, 1])
    for copy in third_group:
        copy.wait_recv()
    acc[...] = mm_t(w_all[...], x_third[...])
    for copy in far_groups[0]:
        copy.wait_recv()
    far_weights = slot_weights(1)
    seen = jnp.maximum(x_main[0, :, 0:EXT].astype(F32), x_main[1, :, 0:EXT].astype(F32))
    seen = jnp.max(seen, axis=0, keepdims=True)
    seen = jnp.max(jnp.where(iota((1, 128), 1) == 3, seen, 0.0), axis=1, keepdims=True)
    over[...] = jnp.broadcast_to(seen, (8, 128))
    over_copies = []
    for q in range(1, SEQ):
        copy = remote(over, over_in.at[q], o_s.at[q], o_r.at[q], y_to(q))
        copy.start()
        over_copies.append(copy)
    third_weights = spread(near_weights, 0) + spread(far_weights, 1)
    finish(1, third_weights[1:2, :])
    for k in FAR[:4]:
        issue(part[k, 2])
    far_forward(1)
    acc[...] = mm_t(w_all[:, 0:step], x_main[1, :, EXT : EXT + step])
    for k in FAR[4:]:
        issue(part[k, 2])
    for k in FAR[:4]:
        issue(part[k, 3])
    far_forward(2)
    far_product(1)
    for k in FAR[4:]:
        issue(part[k, 3])
    far_product(2)
    far_forward(3)
    far_product(3)
    finish(2, far_weights[0:1, :])

    score_copies = []
    for j in range(1, PLANE):
        copy = remote(score, score_in.at[j], ps_s.at[j], ps_r.at[j], p_from(j))
        copy.start()
        score_copies.append(copy)
    place = iota((8, 128), 1)
    gathered = jnp.where(place >> 4 == 0, score[...], 0.0)
    for j in range(1, PLANE):
        score_copies[j - 1].wait_recv()
        gathered = jnp.where(place >> 4 == j, score_in[j], gathered)
    total[...] = gathered
    total_copies = {}
    for k in FAR + (0, 8, 9, 15, 10, 14, 11, 13):
        copy = remote(total, total_in.at[k], zs_s.at[k], zs_r.at[k], z_from(k))
        copy.start()
        total_copies[k] = copy

    restore = hot(natural(iota((block, block), 0)) == iota((block, block), 1))
    for copy in back_copies:
        copy.wait_recv()
    for q in range(SEQ):
        lanes = pl.ds(pl.multiple_of(((s + q) & 3) * block, 128), block)
        for ref, first in ((gg_ref, 0), (gu_ref, 128)):
            value = jnp.concatenate([back[n, q, :, first : first + 128] for n in range(3)], axis=1)
            ref[:, lanes] = mm(value, restore).astype(BF16)

    worst = over[...]
    for q in range(1, SEQ):
        over_copies[q - 1].wait_recv()
        worst = jnp.maximum(worst, over_in[q])
    over_ref[0, 0] = jnp.max(worst).astype(jnp.int32)

    is3 = iota((8, 128), 0) == 1
    low = (place >> 1) & 7
    is_near = iota((8, 128), 0) == 0
    slot = jnp.where(is3, place & 15, jnp.where(is_near, low + 8, low))
    found = jnp.where(slot == SELF, total[...], 0.0)
    for k in FAR + (0, 8, 9, 15, 10, 14, 11, 13):
        total_copies[k].wait_recv()
        found = jnp.where(slot == k, total_in[k], found)
    columns = jnp.transpose(jnp.concatenate([found, jnp.zeros((120, 128), F32)], axis=0))
    row = iota((128, 128), 0)
    j = row >> 4
    target = (((x + (j >> 1)) & 3) << 1) | ((c + (j & 1)) & 1)
    result0 = jnp.zeros((1, 128), F32)
    result1 = jnp.zeros((1, 128), F32)
    for chunk in range(3):
        if chunk == 1:
            k, r = row & 15, jnp.full((128, 128), 2, jnp.int32)
        else:
            k, r = ((row >> 1) & 7) + (8 if chunk == 0 else 0), row & 1
        expert = (((z - 4 - k) & 15) << 3) | target
        first, second = ids0 == expert, ids1 == expert
        match = mm(hot(first | second), earlier) == r.astype(F32)
        column = columns[:, chunk : chunk + 1]
        result0 += jnp.sum(jnp.where(first & match, column, 0.0), axis=0, keepdims=True)
        result1 += jnp.sum(jnp.where(second & match, column, 0.0), axis=0, keepdims=True)
    rg_ref[0:1, :] = result0
    rg_ref[1:2, :] = result1

    for copy in pending + plane_copies + back_copies + score_copies + over_copies:
        copy.wait_send()
    for copy in total_copies.values():
        copy.wait_send()
    for group in y_copies:
        for copy in group:
            copy.wait_send()


def exchange(spare, out_grad, expert_ids, route_weights, down_weight, gate_pre, up_pre):
    tokens, width = out_grad.shape
    ff = down_weight.shape[1]
    rows = gate_pre.shape[1]
    block = rows // SEQ
    wide = width + EXT
    vmem = pl.BlockSpec(memory_space=pltpu.VMEM)
    dma = pltpu.SemaphoreType.DMA
    gate_out, up_out, route, over = pl.pallas_call(
        functools.partial(kernel, spare),
        out_shape=(
            jax.ShapeDtypeStruct((ff, rows), BF16),
            jax.ShapeDtypeStruct((ff, rows), BF16),
            jax.ShapeDtypeStruct((2, tokens), F32),
            jax.ShapeDtypeStruct((1, 1), jnp.int32),
        ),
        in_specs=[vmem, vmem, vmem, pl.BlockSpec(memory_space=pl.ANY), vmem, vmem],
        out_specs=(vmem, vmem, vmem, pl.BlockSpec(memory_space=pltpu.SMEM)),
        scratch_shapes=[
            pltpu.VMEM((256, wide), BF16),
            pltpu.VMEM((256, wide), BF16),
            pltpu.VMEM((256, width // (16 // spare)), BF16),
            pltpu.VMEM((256, width // (16 // spare)), BF16),
            pltpu.VMEM((2, 128, wide), BF16),
            pltpu.VMEM((2, 128, wide), BF16),
            pltpu.VMEM((128, width), BF16),
            pltpu.VMEM((128, width), BF16),
            pltpu.VMEM((SEQ * ff, width), BF16),
            pltpu.VMEM((SEQ * ff, block), BF16),
            pltpu.VMEM((SEQ * ff, block), BF16),
            pltpu.VMEM((SEQ * ff, block), BF16),
            pltpu.VMEM((SEQ * ff, block), BF16),
            pltpu.VMEM((SEQ * ff, 128), F32),
            pltpu.VMEM((3, SEQ * ff, 256), BF16),
            pltpu.VMEM((3, SEQ, ff, 256), BF16),
            pltpu.VMEM((8, 128), F32),
            pltpu.VMEM((PLANE, 8, 128), F32),
            pltpu.VMEM((8, 128), F32),
            pltpu.VMEM((ZN, 8, 128), F32),
            pltpu.VMEM((8, 128), F32),
            pltpu.VMEM((SEQ, 8, 128), F32),
            dma((ZN, 5)), dma((ZN, 5)), dma((ZN,)), dma((ZN,)),
            dma((6, PLANE)), dma((6, PLANE)), dma((3, SEQ)), dma((3, SEQ)),
            dma((3, SEQ)), dma((3, SEQ)), dma((PLANE,)), dma((PLANE,)),
            dma((ZN,)), dma((ZN,)), dma((SEQ,)), dma((SEQ,)), dma,
        ],
        compiler_params=pltpu.CompilerParams(
            collective_id=0 if spare == 4 else 1, has_side_effects=True, vmem_limit_bytes=56 * 2**20
        ),
        cost_estimate=pl.CostEstimate(
            flops=2 * SEQ * ff * width * block, bytes_accessed=8 * 2**20, transcendentals=0
        ),
        name="expert_backward_%d" % spare,
    )(
        out_grad,
        expert_ids.T,
        route_weights.T,
        down_weight[0],
        gate_pre[0].T,
        up_pre[0].T,
    )
    return gate_out, up_out, route, over


def per_device(*arrays):
    gate_out, up_out, route, over = exchange(4, *arrays)
    gate_out, up_out, route = lax.cond(
        over[0, 0] > 0,
        lambda: exchange(8, *arrays)[:3],
        lambda: (gate_out, up_out, route),
    )
    return gate_out.T[None], up_out.T[None], route.T


def solution(mesh):
    placed = (
        P(("seq", "exp"), None),
        P(("seq", "exp"), None),
        P(("seq", "exp"), None),
        P("exp", "seq", None),
        P("exp", None, "seq"),
        P("exp", None, "seq"),
    )
    return jax.shard_map(
        per_device,
        mesh=mesh,
        in_specs=placed,
        out_specs=(P("exp", None, "seq"), P("exp", None, "seq"), P(("seq", "exp"), None)),
        check_vma=False,
    )
```

```python
import functools

import jax
import jax.numpy as jnp
from jax import lax
from jax.experimental import pallas as pl
from jax.experimental.pallas import tpu as pltpu
from jax.sharding import PartitionSpec as P

MESH = pl.DeviceIdType.MESH
WINDOW = 8
PIECES = (1408, 1152, 1024, 512)
SEQ, ZN, PLANE = 4, 16, 8
SELF = 12
EXT = 128
F32, BF16 = jnp.float32, jnp.bfloat16
FAR = (4, 3, 5, 2, 6, 1, 7)
ALL_THIRD = (4, 3, 5, 2, 6, 1, 7, 0, 8, 9, 15, 10, 14, 11, 13)


def iota(shape, dim):
    return lax.broadcasted_iota(jnp.int32, shape, dim)


def hot(cond):
    return jnp.where(cond, 1.0, 0.0).astype(BF16)


def mm(a, b):
    return jnp.dot(a, b, preferred_element_type=F32)


def mm_t(a, b):
    return lax.dot_general(a, b, (((1,), (1,)), ((), ())), preferred_element_type=F32)


def kernel(
    spare, x_hbm, ids_ref, rw_ref, w_hbm, g_hbm, u_hbm,
    gg_ref, gu_ref, rg_ref, over_ref,
    x_ref, g_ref, u_ref, s_main, r_main, s_third, r_third, t_main, x_main, t_third, x_third,
    w_all, g_all, u_all, g_perm, u_perm, factors, restore, owner, acc, grads, back,
    score, score_in, total, total_in, over, over_in,
    z_s, z_r, zt_s, zt_r, p_s, p_r, y_s, y_r, b_s, b_r, ps_s, ps_r, zs_s, zs_r, o_s, o_r, local_sem,
):
    width = x_ref.shape[1]
    ff = w_hbm.shape[0]
    block = g_ref.shape[1] // SEQ
    wide = width + EXT
    parts = 16 // spare
    span3 = width // parts
    pieces = [(EXT + sum(PIECES[:n]), size) for n, size in enumerate(PIECES)]

    s = lax.axis_index("seq")
    e = lax.axis_index("exp")
    z, x, c = e >> 3, (e >> 1) & 3, e & 1

    def z_to(k):
        return (s, (((z - 4 - k) & 15) << 3) | (e & 7))

    def z_from(k):
        return (s, (((z + 4 + k) & 15) << 3) | (e & 7))

    def p_to(j):
        return (s, (z << 3) | (((x + (j >> 1)) & 3) << 1) | ((c + (j & 1)) & 1))

    def p_from(j):
        return (s, (z << 3) | (((x - (j >> 1)) & 3) << 1) | ((c + (j & 1)) & 1))

    def y_to(q):
        return ((s + q) & 3, e)

    def y_from(q):
        return ((s - q) & 3, e)

    def remote(src, dst, send, recv, device):
        return pltpu.make_async_remote_copy(
            src_ref=src, dst_ref=dst, send_sem=send, recv_sem=recv,
            device_id=device, device_id_type=MESH,
        )

    barrier = pltpu.get_barrier_semaphore()
    for k in range(ZN):
        if k != SELF:
            pl.semaphore_signal(barrier, inc=1, device_id=z_from(k), device_id_type=MESH)
    for j in range(1, PLANE):
        pl.semaphore_signal(barrier, inc=1, device_id=p_from(j), device_id_type=MESH)
    for q in range(1, SEQ):
        pl.semaphore_signal(barrier, inc=1, device_id=y_from(q), device_id_type=MESH)

    own = [
        pltpu.make_async_copy(src, dst, local_sem.at[n])
        for n, (src, dst) in enumerate(
            ((x_hbm, x_ref), (w_hbm, w_all.at[pl.ds(0, ff)]), (g_hbm, g_ref), (u_hbm, u_ref))
        )
    ]
    for copy in own:
        copy.start()

    ids0, ids1 = ids_ref[0:1, :], ids_ref[1:2, :]
    w0, w1 = rw_ref[0:1, :].astype(F32), rw_ref[1:2, :].astype(F32)
    tokens = ids_ref.shape[1]
    earlier = hot(iota((tokens, tokens), 0) < iota((tokens, tokens), 1))
    row = iota((256, tokens), 0)
    lane = iota((256, tokens), 1)
    expert = (((z - 4 - (row >> 4)) & 15) << 3) | (row & 7)
    upper = (row >> 3) & 1
    named0 = ids0 == expert
    named = named0 | (ids1 == expert)
    rank = mm(hot(named), earlier)
    is_main = named & (rank == upper.astype(F32))
    is_third = named & (rank == 2.0)
    m_main = hot(is_main)
    m_third = hot(is_third)
    have = mm_t(jnp.ones((16, tokens), BF16), m_third)
    src, dst = iota((256, 256), 0), iota((256, 256), 1)
    before = (src >> 4 == dst >> 4) & (src & 8 == 0)
    ahead = mm(have.astype(BF16), hot(before & (src & 7 < dst & 7)))
    held = mm(have.astype(BF16), hot(before))
    excess = jnp.max(jnp.where(held > spare, 1.0, 0.0))
    packed = (src >> 4 == dst >> 4) & (dst & 8 == 0)
    packed = packed & (ahead[0:1, :] == (src & (spare - 1)).astype(F32))
    m_packed = mm(hot(packed), m_third)
    part_of = (row & 15) >> (spare.bit_length() - 1)
    m_part = [hot((m_packed > 0.5) & (part_of == n)) for n in range(parts)]
    rank_in = mm(hot((src >> 4 == dst >> 4) & (dst & 8 == 0) & (dst & 7 < src & 7)), m_third)
    v_spot = jnp.sum(rank_in, axis=1, keepdims=True)
    v_have = jnp.sum(m_third.astype(F32), axis=1, keepdims=True)
    v_spot = jnp.where((v_have > 0.5) & (v_spot < spare - 0.5), v_spot + 1.0, 0.0)
    value = jnp.where(named0, w0, w1)
    v_main = jnp.sum(jnp.where(is_main, value, 0.0), axis=1, keepdims=True)
    v_third = jnp.sum(jnp.where(is_third, value, 0.0), axis=1, keepdims=True)
    s_main[:, 0:EXT] = jnp.where(
        lane == 0,
        v_main,
        jnp.where(lane == 1, v_third, jnp.where(lane == 2, v_spot, jnp.where(lane == 3, excess, 0.0))),
    ).astype(BF16)

    score[...] = jnp.zeros((8, 128), F32)
    own[0].wait()
    for start in range(0, width, 1024):
        s_main[128:256, EXT + start : EXT + start + 1024] = mm(
            m_main[128:256], x_ref[:, start : start + 1024]
        ).astype(BF16)
    for copy in own[1:]:
        copy.wait()
    pl.semaphore_wait(barrier, ZN - 1 + PLANE - 1 + SEQ - 1)

    y_copies = []
    for q in range(1, SEQ):
        rows = pl.ds(ff * q, ff)
        lanes = pl.ds(pl.multiple_of(((s + q) & 3) * block, 128), block)
        y_copies.append([
            remote(g_ref.at[:, lanes], g_all.at[rows], y_s.at[0, q], y_r.at[0, q], y_to(q)),
            remote(u_ref.at[:, lanes], u_all.at[rows], y_s.at[1, q], y_r.at[1, q], y_to(q)),
            remote(w_all.at[pl.ds(0, ff)], w_all.at[rows], y_s.at[2, q], y_r.at[2, q], y_to(q)),
        ])

    pending = []

    def issue(copy):
        if len(pending) >= WINDOW:
            pending.pop(0).wait_send()
        copy.start()
        pending.append(copy)

    def main_copy(k, start, size, n):
        part = (pl.ds(16 * k, 16), pl.ds(start, size))
        return remote(s_main.at[part], r_main.at[part], z_s.at[k, n], z_r.at[k, n], z_to(k))

    whole = {k: main_copy(k, 0, wide, 0) for k in (8, 9, 15, 10, 14, 11, 13, 0)}
    part = {
        (k, n): main_copy(k, start if n else 0, size if n else EXT + size, n)
        for n, (start, size) in enumerate(pieces)
        for k in FAR
    }
    third = {
        k: remote(
            s_third.at[pl.ds(16 * k, 16)], r_third.at[pl.ds(16 * k, 16)],
            zt_s.at[k], zt_r.at[k], z_to(k),
        )
        for k in ALL_THIRD
    }

    for k in (8, 9, 15, 10, 14):
        issue(whole[k])
    for n in (0, 1, 2):
        for q in range(1, SEQ):
            y_copies[q - 1][n].start()
    for start in range(0, width, 1024):
        s_main[0:128, EXT + start : EXT + start + 1024] = mm(
            m_main[0:128], x_ref[:, start : start + 1024]
        ).astype(BF16)
    packed_rows = mm(m_part[0], x_ref[:, 0:span3])
    for n in range(1, parts):
        packed_rows += mm(m_part[n], x_ref[:, span3 * n : span3 * n + span3])
    s_third[...] = packed_rows.astype(BF16)
    for k in (0, 11, 13):
        issue(whole[k])
    r_main[16 * SELF : 16 * SELF + 16, :] = s_main[16 * SELF : 16 * SELF + 16, :]
    r_third[16 * SELF : 16 * SELF + 16, :] = s_third[16 * SELF : 16 * SELF + 16, :]

    out_row = iota((128, 128), 0)
    j_of = out_row >> 4
    p_of = (((x + (j_of >> 1)) & 3) << 1) | ((c + (j_of & 1)) & 1)
    regroup = hot(
        iota((128, 128), 1) == ((out_row >> 1) & 7) * 16 + (out_row & 1) * 8 + p_of
    )
    plane_copies = []

    def plane_send(src, dst, start, size, n):
        group = []
        for j in range(1, PLANE):
            area = (pl.ds(16 * j, 16), pl.ds(start, size))
            copy = remote(src.at[area], dst.at[area], p_s.at[n, j], p_r.at[n, j], p_to(j))
            copy.start()
            group.append(copy)
        plane_copies.extend(group)
        dst[0:16, start : start + size] = src[0:16, start : start + size]
        return group

    def split(start, size):
        at = start
        while at < start + size:
            span = min(1152, start + size - at)
            yield at, span
            at += span

    def main_forward(h, start, size, n):
        base = 128 if h == 0 else 0
        for at, span in split(start, size):
            t_main[h, :, at : at + span] = mm(
                regroup, r_main[base : base + 128, at : at + span]
            ).astype(BF16)
        return plane_send(t_main.at[h], x_main.at[h], start, size, n)

    def third_forward(n):
        out_row = iota((128, 256), 0)
        column = iota((128, 256), 1)
        j = out_row >> 4
        p = (((x + (j >> 1)) & 3) << 1) | ((c + (j & 1)) & 1)
        chosen = mm(hot(column == (out_row & 15) * 16 + p), r_main[:, 0:EXT])
        spot = chosen[:, 2:3] - 1.0
        spot = (out_row & 15 == column >> 4) & (spot == (column & (spare - 1)).astype(F32))
        part_of = (column & 15) >> (spare.bit_length() - 1)
        for m in range(parts):
            match = hot(spot & (part_of == m))
            t_third[:, span3 * m : span3 * m + span3] = mm(match, r_third[...]).astype(BF16)
        return plane_send(t_third, x_third, 0, width, n)

    def natural(index):
        chunk, low = index >> 7, index & 127
        j = low >> 4
        is3 = chunk == 1
        k = jnp.where(is3, low & 15, ((low >> 1) & 7) + jnp.where(chunk == 0, 8, 0))
        r = jnp.where(is3, 2, low & 1)
        source = (((x - (j >> 1)) & 3) << 1) | ((c + (j & 1)) & 1)
        return ((z + 4 + k) & 15) * 24 + source * 3 + r

    def gates_ready():
        own = pl.ds(pl.multiple_of(s * block, 128), block)
        g_all[0:ff, :] = g_ref[:, own]
        u_all[0:ff, :] = u_ref[:, own]
        order = hot(iota((block, block), 0) == natural(iota((block, block), 1)))
        for q in range(SEQ):
            if q:
                y_copies[q - 1][0].wait_recv()
                y_copies[q - 1][1].wait_recv()
            rows = slice(ff * q, ff * q + ff)
            g_perm[rows, :] = mm(g_all[rows, :], order).astype(BF16)
            u_perm[rows, :] = mm(u_all[rows, :], order).astype(BF16)

    def orders():
        restore[...] = hot(natural(iota((block, block), 0)) == iota((block, block), 1))
        row = iota((128, 128), 0)
        j = row >> 4
        target = (((x + (j >> 1)) & 3) << 1) | ((c + (j & 1)) & 1)
        for chunk in range(3):
            if chunk == 1:
                k, r = row & 15, jnp.full((128, 128), 2, jnp.int32)
            else:
                k, r = ((row >> 1) & 7) + (8 if chunk == 0 else 0), row & 1
            expert = (((z - 4 - k) & 15) << 3) | target
            first, second = ids0 == expert, ids1 == expert
            match = mm(hot(first | second), earlier) == r.astype(F32)
            owner[chunk, 0] = hot(first & match)
            owner[chunk, 1] = hot(second & match)

    def prepare(chunk):
        lanes = slice(128 * chunk, 128 * chunk + 128)
        for q in range(SEQ):
            rows = slice(ff * q, ff * q + ff)
            gate = g_perm[rows, lanes].astype(F32)
            up = u_perm[rows, lanes].astype(F32)
            sig = jax.nn.sigmoid(gate)
            activated = gate * sig
            factors[0, rows, :] = activated
            factors[1, rows, :] = activated * up
            factors[2, rows, :] = up * sig * (1.0 + gate * (1.0 - sig))

    back_copies = []

    def finish(chunk, weights, cols=None):
        summed = jnp.zeros((1, 128), F32)
        for q in (2, 1, 3, 0):
            rows = slice(ff * q, ff * q + ff)
            projected = acc[rows, :]
            if cols is not None:
                projected += mm_t(
                    w_all[rows, cols[0] : cols[0] + cols[1]],
                    x_main[1, :, EXT + cols[0] : EXT + cols[0] + cols[1]],
                )
            summed = summed + jnp.sum(factors[1, rows, :] * projected, axis=0, keepdims=True)
            scaled = weights * projected
            grad_up = (scaled * factors[0, rows, :]).astype(BF16)
            grad_gate = (scaled * factors[2, rows, :]).astype(BF16)
            if q:
                grads[chunk, rows, 0:128] = grad_gate
                grads[chunk, rows, 128:256] = grad_up
                copy = remote(
                    grads.at[chunk, pl.ds(ff * q, ff)], back.at[chunk, q],
                    b_s.at[chunk, q], b_r.at[chunk, q], y_from(q),
                )
                copy.start()
                back_copies.append(copy)
            else:
                back[chunk, 0, :, 0:128] = grad_gate
                back[chunk, 0, :, 128:256] = grad_up
        score[chunk : chunk + 1, :] = summed

    def slot_weights(h):
        pick = hot(iota((16, 128), 0) == iota((16, 128), 1))
        return mm_t(pick, x_main[h, :, 0:EXT])

    def spread(weights, h):
        src, dst = iota((128, 128), 0), iota((128, 128), 1)
        match = (src & 1 == 0) & (src >> 4 == dst >> 4)
        match = match & (dst & 15 == ((src >> 1) & 7) + (8 if h == 0 else 0))
        return mm(weights.astype(BF16), hot(match))

    for k in FAR[:4]:
        issue(part[k, 0])
    for k in (8, 9, 15, 10, 14, 11, 13):
        whole[k].wait_recv()
    near_group = main_forward(0, 0, wide, 0)
    for k in FAR[4:]:
        issue(part[k, 0])
    for k in ALL_THIRD[:9]:
        issue(third[k])
    gates_ready()
    prepare(0)
    far_groups = []

    def far_forward(n):
        for k in FAR:
            part[k, n].wait_recv()
        start, size = pieces[n]
        if n == 0:
            start, size = 0, EXT + size
        far_groups.append(main_forward(1, start, size, 2 + n))

    def far_product(n):
        for copy in far_groups[n]:
            copy.wait_recv()
        start, size = pieces[n]
        return mm_t(w_all[:, start - EXT : start - EXT + size], x_main[1, :, start : start + size])

    for k in ALL_THIRD[9:]:
        issue(third[k])
    whole[0].wait_recv()
    far_forward(0)
    for k in FAR[:4]:
        issue(part[k, 1])
    orders()
    for k in ALL_THIRD:
        third[k].wait_recv()
    third_group = third_forward(1)
    for k in FAR[4:]:
        issue(part[k, 1])
    for group in y_copies:
        group[2].wait_recv()
    for copy in near_group:
        copy.wait_recv()
    acc[...] = mm_t(w_all[...], x_main[0, :, EXT:])
    near_weights = slot_weights(0)
    finish(0, near_weights[0:1, :])
    for k in FAR[:4]:
        issue(part[k, 2])
    far_forward(1)
    for k in FAR[4:]:
        issue(part[k, 2])
    for copy in third_group:
        copy.wait_recv()
    prepare(1)
    acc[...] = mm_t(w_all[...], x_third[...])
    for k in FAR:
        issue(part[k, 3])
    for copy in far_groups[0]:
        copy.wait_recv()
    far_weights = slot_weights(1)
    seen = jnp.maximum(x_main[0, :, 0:EXT].astype(F32), x_main[1, :, 0:EXT].astype(F32))
    seen = jnp.max(seen, axis=0, keepdims=True)
    seen = jnp.max(jnp.where(iota((1, 128), 1) == 3, seen, 0.0), axis=1, keepdims=True)
    over[...] = jnp.broadcast_to(seen, (8, 128))
    over_copies = []
    for q in range(1, SEQ):
        copy = remote(over, over_in.at[q], o_s.at[q], o_r.at[q], y_to(q))
        copy.start()
        over_copies.append(copy)
    third_weights = spread(near_weights, 0) + spread(far_weights, 1)
    finish(1, third_weights[1:2, :])
    prepare(2)
    start, size = pieces[0]
    acc[...] = mm_t(w_all[:, 0:size], x_main[1, :, start : start + size])
    far_forward(2)
    acc[...] += far_product(1)

    def restored(q, chunks, first):
        value = jnp.concatenate([back[n, q, :, first : first + 128] for n in chunks], axis=1)
        return mm(value, restore[128 * chunks[0] : 128 * chunks[-1] + 128, :])

    def home(q):
        return pl.ds(pl.multiple_of(((s + q) & 3) * block, 128), block)

    far_forward(3)
    for copy in back_copies:
        copy.wait_recv()
    early = len(back_copies)
    for q in range(SEQ):
        gg_ref[:, home(q)] = restored(q, (0, 1), 0).astype(BF16)
        gu_ref[:, home(q)] = restored(q, (0, 1), 128).astype(BF16)
    acc[...] += far_product(2)
    for copy in far_groups[3]:
        copy.wait_recv()
    finish(2, far_weights[0:1, :], (pieces[3][0] - EXT, pieces[3][1]))

    score_copies = []
    for j in range(1, PLANE):
        copy = remote(score, score_in.at[j], ps_s.at[j], ps_r.at[j], p_from(j))
        copy.start()
        score_copies.append(copy)
    place = iota((8, 128), 1)
    gathered = jnp.where(place >> 4 == 0, score[...], 0.0)
    for j in range(1, PLANE):
        score_copies[j - 1].wait_recv()
        gathered = jnp.where(place >> 4 == j, score_in[j], gathered)
    total[...] = gathered
    total_copies = {}
    for k in FAR + (0, 8, 9, 15, 10, 14, 11, 13):
        copy = remote(total, total_in.at[k], zs_s.at[k], zs_r.at[k], z_from(k))
        copy.start()
        total_copies[k] = copy

    for copy in back_copies[early:]:
        copy.wait_recv()
    for q in (0, 1, 3, 2):
        for ref, first in ((gg_ref, 0), (gu_ref, 128)):
            ref[:, home(q)] = (ref[:, home(q)].astype(F32) + restored(q, (2,), first)).astype(BF16)
    worst = over[...]
    for q in range(1, SEQ):
        over_copies[q - 1].wait_recv()
        worst = jnp.maximum(worst, over_in[q])
    over_ref[0, 0] = jnp.max(worst).astype(jnp.int32)

    is3 = iota((8, 128), 0) == 1
    low = (place >> 1) & 7
    is_near = iota((8, 128), 0) == 0
    slot = jnp.where(is3, place & 15, jnp.where(is_near, low + 8, low))
    found = jnp.where(slot == SELF, total[...], 0.0)
    for k in FAR + (0, 8, 9, 15, 10, 14, 11, 13):
        total_copies[k].wait_recv()
        found = jnp.where(slot == k, total_in[k], found)
    columns = jnp.transpose(jnp.concatenate([found, jnp.zeros((120, 128), F32)], axis=0))
    result0 = jnp.zeros((1, 128), F32)
    result1 = jnp.zeros((1, 128), F32)
    for chunk in range(3):
        column = columns[:, chunk : chunk + 1]
        result0 += jnp.sum(jnp.where(owner[chunk, 0] > 0.5, column, 0.0), axis=0, keepdims=True)
        result1 += jnp.sum(jnp.where(owner[chunk, 1] > 0.5, column, 0.0), axis=0, keepdims=True)
    rg_ref[0:1, :] = result0
    rg_ref[1:2, :] = result1

    for copy in pending + plane_copies + back_copies + score_copies + over_copies:
        copy.wait_send()
    for copy in total_copies.values():
        copy.wait_send()
    for group in y_copies:
        for copy in group:
            copy.wait_send()


def exchange(spare, out_grad, expert_ids, route_weights, down_weight, gate_pre, up_pre):
    tokens, width = out_grad.shape
    ff = down_weight.shape[1]
    rows = gate_pre.shape[1]
    block = rows // SEQ
    wide = width + EXT
    vmem = pl.BlockSpec(memory_space=pltpu.VMEM)
    hbm = pl.BlockSpec(memory_space=pl.ANY)
    dma = pltpu.SemaphoreType.DMA
    gate_out, up_out, route, over = pl.pallas_call(
        functools.partial(kernel, spare),
        out_shape=(
            jax.ShapeDtypeStruct((ff, rows), BF16),
            jax.ShapeDtypeStruct((ff, rows), BF16),
            jax.ShapeDtypeStruct((2, tokens), F32),
            jax.ShapeDtypeStruct((1, 1), jnp.int32),
        ),
        in_specs=[hbm, vmem, vmem, hbm, hbm, hbm],
        out_specs=(vmem, vmem, vmem, pl.BlockSpec(memory_space=pltpu.SMEM)),
        scratch_shapes=[
            pltpu.VMEM((tokens, width), BF16),
            pltpu.VMEM((ff, rows), BF16),
            pltpu.VMEM((ff, rows), BF16),
            pltpu.VMEM((256, wide), BF16),
            pltpu.VMEM((256, wide), BF16),
            pltpu.VMEM((256, width // (16 // spare)), BF16),
            pltpu.VMEM((256, width // (16 // spare)), BF16),
            pltpu.VMEM((2, 128, wide), BF16),
            pltpu.VMEM((2, 128, wide), BF16),
            pltpu.VMEM((128, width), BF16),
            pltpu.VMEM((128, width), BF16),
            pltpu.VMEM((SEQ * ff, width), BF16),
            pltpu.VMEM((SEQ * ff, block), BF16),
            pltpu.VMEM((SEQ * ff, block), BF16),
            pltpu.VMEM((SEQ * ff, block), BF16),
            pltpu.VMEM((SEQ * ff, block), BF16),
            pltpu.VMEM((3, SEQ * ff, 128), F32),
            pltpu.VMEM((block, block), BF16),
            pltpu.VMEM((3, 2, 128, tokens), BF16),
            pltpu.VMEM((SEQ * ff, 128), F32),
            pltpu.VMEM((3, SEQ * ff, 256), BF16),
            pltpu.VMEM((3, SEQ, ff, 256), BF16),
            pltpu.VMEM((8, 128), F32),
            pltpu.VMEM((PLANE, 8, 128), F32),
            pltpu.VMEM((8, 128), F32),
            pltpu.VMEM((ZN, 8, 128), F32),
            pltpu.VMEM((8, 128), F32),
            pltpu.VMEM((SEQ, 8, 128), F32),
            dma((ZN, 4)), dma((ZN, 4)), dma((ZN,)), dma((ZN,)),
            dma((6, PLANE)), dma((6, PLANE)), dma((3, SEQ)), dma((3, SEQ)),
            dma((3, SEQ)), dma((3, SEQ)), dma((PLANE,)), dma((PLANE,)),
            dma((ZN,)), dma((ZN,)), dma((SEQ,)), dma((SEQ,)), dma((4,)),
        ],
        compiler_params=pltpu.CompilerParams(
            collective_id=0 if spare == 4 else 1, has_side_effects=True, vmem_limit_bytes=56 * 2**20
        ),
        cost_estimate=pl.CostEstimate(
            flops=2 * SEQ * ff * width * block, bytes_accessed=8 * 2**20, transcendentals=0
        ),
        name="expert_backward_%d" % spare,
    )(
        out_grad,
        expert_ids.T,
        route_weights.T,
        down_weight[0],
        gate_pre[0].T,
        up_pre[0].T,
    )
    return gate_out, up_out, route, over


def per_device(*arrays):
    gate_out, up_out, route, over = exchange(4, *arrays)
    gate_out, up_out, route = lax.cond(
        over[0, 0] > 0,
        lambda: exchange(8, *arrays)[:3],
        lambda: (gate_out, up_out, route),
    )
    return gate_out.T[None], up_out.T[None], route.T


def solution(mesh):
    placed = (
        P(("seq", "exp"), None),
        P(("seq", "exp"), None),
        P(("seq", "exp"), None),
        P("exp", "seq", None),
        P("exp", None, "seq"),
        P("exp", None, "seq"),
    )
    return jax.shard_map(
        per_device,
        mesh=mesh,
        in_specs=placed,
        out_specs=(P("exp", None, "seq"), P("exp", None, "seq"), P(("seq", "exp"), None)),
        check_vma=False,
    )
```

```python
import functools

import jax
import jax.numpy as jnp
from jax import lax
from jax.experimental import pallas as pl
from jax.experimental.pallas import tpu as pltpu
from jax.sharding import PartitionSpec as P

MESH = pl.DeviceIdType.MESH
WINDOW = 14
PIECES = (1408, 1152, 1024, 512)
SEQ, ZN, PLANE = 4, 16, 8
SELF = 12
EXT = 128
F32, BF16 = jnp.float32, jnp.bfloat16
FAR = (4, 3, 5, 2, 6, 1, 7)
ALL_THIRD = (4, 3, 5, 2, 6, 1, 7, 0, 8, 9, 15, 10, 14, 11, 13)


def iota(shape, dim):
    return lax.broadcasted_iota(jnp.int32, shape, dim)


def hot(cond):
    return jnp.where(cond, 1.0, 0.0).astype(BF16)


def mm(a, b):
    return jnp.dot(a, b, preferred_element_type=F32)


def mm_t(a, b):
    return lax.dot_general(a, b, (((1,), (1,)), ((), ())), preferred_element_type=F32)


def kernel(
    spare, x_hbm, ids_ref, rw_ref, w_hbm, g_hbm, u_hbm,
    gg_ref, gu_ref, rg_ref, over_ref,
    x_ref, g_ref, u_ref, s_main, r_main, s_third, r_third, t_main, x_main, t_third, x_third,
    w_all, g_all, u_all, g_perm, u_perm, factors, restore, owner, acc, grads, back,
    score, score_in, total, total_in, over, over_in,
    z_s, z_r, zt_s, zt_r, p_s, p_r, y_s, y_r, b_s, b_r, ps_s, ps_r, zs_s, zs_r, o_s, o_r, local_sem,
):
    width = x_ref.shape[1]
    ff = w_hbm.shape[0]
    block = g_ref.shape[1] // SEQ
    parts = 16 // spare
    span3 = width // parts
    pieces = [(sum(PIECES[:n]), size) for n, size in enumerate(PIECES)]

    s = lax.axis_index("seq")
    e = lax.axis_index("exp")
    z, x, c = e >> 3, (e >> 1) & 3, e & 1

    def z_to(k):
        return (s, (((z - 4 - k) & 15) << 3) | (e & 7))

    def z_from(k):
        return (s, (((z + 4 + k) & 15) << 3) | (e & 7))

    def p_to(j):
        return (s, (z << 3) | (((x + (j >> 1)) & 3) << 1) | ((c + (j & 1)) & 1))

    def p_from(j):
        return (s, (z << 3) | (((x - (j >> 1)) & 3) << 1) | ((c + (j & 1)) & 1))

    def y_to(q):
        return ((s + q) & 3, e)

    def y_from(q):
        return ((s - q) & 3, e)

    def remote(src, dst, send, recv, device):
        return pltpu.make_async_remote_copy(
            src_ref=src, dst_ref=dst, send_sem=send, recv_sem=recv,
            device_id=device, device_id_type=MESH,
        )

    barrier = pltpu.get_barrier_semaphore()
    for k in range(ZN):
        if k != SELF:
            pl.semaphore_signal(barrier, inc=1, device_id=z_from(k), device_id_type=MESH)
    for j in range(1, PLANE):
        pl.semaphore_signal(barrier, inc=1, device_id=p_from(j), device_id_type=MESH)
    for q in range(1, SEQ):
        pl.semaphore_signal(barrier, inc=1, device_id=y_from(q), device_id_type=MESH)

    own = [
        pltpu.make_async_copy(src, dst, local_sem.at[n])
        for n, (src, dst) in enumerate(
            ((x_hbm, x_ref), (w_hbm, w_all.at[pl.ds(0, ff)]), (g_hbm, g_ref), (u_hbm, u_ref))
        )
    ]
    for copy in own:
        copy.start()

    ids0, ids1 = ids_ref[0:1, :], ids_ref[1:2, :]
    w0, w1 = rw_ref[0:1, :].astype(F32), rw_ref[1:2, :].astype(F32)
    tokens = ids_ref.shape[1]
    earlier = hot(iota((tokens, tokens), 0) < iota((tokens, tokens), 1))
    row = iota((256, tokens), 0)
    lane = iota((256, tokens), 1)
    expert = (((z - 4 - (row >> 4)) & 15) << 3) | (row & 7)
    upper = (row >> 3) & 1
    named0 = ids0 == expert
    named = named0 | (ids1 == expert)
    rank = mm(hot(named), earlier)
    is_main = named & (rank == upper.astype(F32))
    is_third = named & (rank == 2.0)
    m_main = hot(is_main)
    score[...] = jnp.zeros((8, 128), F32)
    own[0].wait()
    for start in range(0, width, 1024):
        s_main[128:256, start : start + 1024] = mm(
            m_main[128:256], x_ref[:, start : start + 1024]
        ).astype(BF16)
    for copy in own[1:]:
        copy.wait()
    pl.semaphore_wait(barrier, ZN - 1 + PLANE - 1 + SEQ - 1)

    y_copies = []
    for q in range(1, SEQ):
        rows = pl.ds(ff * q, ff)
        lanes = pl.ds(pl.multiple_of(((s + q) & 3) * block, 128), block)
        y_copies.append([
            remote(g_ref.at[:, lanes], g_all.at[rows], y_s.at[0, q], y_r.at[0, q], y_to(q)),
            remote(u_ref.at[:, lanes], u_all.at[rows], y_s.at[1, q], y_r.at[1, q], y_to(q)),
            remote(w_all.at[pl.ds(0, ff)], w_all.at[rows], y_s.at[2, q], y_r.at[2, q], y_to(q)),
        ])

    pending, background = [], []

    def issue(copy):
        if len(pending) >= WINDOW:
            pending.pop(0).wait_send()
        copy.start()
        pending.append(copy)
        if background:
            background.pop(0).start()

    def flush():
        while background:
            background.pop(0).start()

    def main_copy(k, start, size, n):
        part = (pl.ds(16 * k, 16), pl.ds(start, size))
        return remote(s_main.at[part], r_main.at[part], z_s.at[k, n], z_r.at[k, n], z_to(k))

    whole = {k: main_copy(k, 0, width, 0) for k in (8, 9, 15, 10, 14, 11, 13, 0)}
    part = {
        (k, n): main_copy(k, start, size, n) for n, (start, size) in enumerate(pieces) for k in FAR
    }
    third = {
        k: remote(
            s_third.at[pl.ds(16 * k, 16)], r_third.at[pl.ds(16 * k, 16)],
            zt_s.at[k], zt_r.at[k], z_to(k),
        )
        for k in ALL_THIRD
    }

    for k in (8, 9, 15, 10, 14, 11, 13):
        issue(whole[k])
    for n in (0, 1, 2):
        for q in range(1, SEQ):
            y_copies[q - 1][n].start()
    for start in range(0, width, 1024):
        s_main[0:128, start : start + 1024] = mm(
            m_main[0:128], x_ref[:, start : start + 1024]
        ).astype(BF16)
    issue(whole[0])
    for k in FAR[:3]:
        issue(part[k, 0])

    m_third = hot(is_third)
    have = mm_t(jnp.ones((16, tokens), BF16), m_third)
    src, dst = iota((256, 256), 0), iota((256, 256), 1)
    before = (src >> 4 == dst >> 4) & (src & 8 == 0)
    ahead = mm(have.astype(BF16), hot(before & (src & 7 < dst & 7)))
    held = mm(have.astype(BF16), hot(before))
    excess = jnp.max(jnp.where(held > spare, 1.0, 0.0))
    packed = (src >> 4 == dst >> 4) & (dst & 8 == 0)
    packed = packed & (ahead[0:1, :] == (src & (spare - 1)).astype(F32))
    m_packed = mm(hot(packed), m_third)
    part_of = (row & 15) >> (spare.bit_length() - 1)
    m_part = [hot((m_packed > 0.5) & (part_of == n)) for n in range(parts)]
    rank_in = mm(hot((src >> 4 == dst >> 4) & (dst & 8 == 0) & (dst & 7 < src & 7)), m_third)
    v_spot = jnp.sum(rank_in, axis=1, keepdims=True)
    v_have = jnp.sum(m_third.astype(F32), axis=1, keepdims=True)
    v_spot = jnp.where((v_have > 0.5) & (v_spot < spare - 0.5), v_spot + 1.0, 0.0)
    value = jnp.where(named0, w0, w1)
    v_main = jnp.sum(jnp.where(is_main, value, 0.0), axis=1, keepdims=True)
    v_third = jnp.sum(jnp.where(is_third, value, 0.0), axis=1, keepdims=True)
    s_third[:, 0:EXT] = jnp.where(
        lane == 0,
        v_main,
        jnp.where(lane == 1, v_third, jnp.where(lane == 2, v_spot, jnp.where(lane == 3, excess, 0.0))),
    ).astype(BF16)

    packed_rows = mm(m_part[0], x_ref[:, 0:span3])
    for n in range(1, parts):
        packed_rows += mm(m_part[n], x_ref[:, span3 * n : span3 * n + span3])
    s_third[:, EXT:] = packed_rows.astype(BF16)
    r_main[16 * SELF : 16 * SELF + 16, :] = s_main[16 * SELF : 16 * SELF + 16, :]
    r_third[16 * SELF : 16 * SELF + 16, :] = s_third[16 * SELF : 16 * SELF + 16, :]

    out_row = iota((128, 128), 0)
    j_of = out_row >> 4
    p_of = (((x + (j_of >> 1)) & 3) << 1) | ((c + (j_of & 1)) & 1)
    regroup = hot(
        iota((128, 128), 1) == ((out_row >> 1) & 7) * 16 + (out_row & 1) * 8 + p_of
    )
    plane_copies = []

    def plane_send(src, dst, start, size, n):
        group = []
        for j in range(1, PLANE):
            area = (pl.ds(16 * j, 16), pl.ds(start, size))
            copy = remote(src.at[area], dst.at[area], p_s.at[n, j], p_r.at[n, j], p_to(j))
            group.append(copy)
        plane_copies.extend(group)
        background.extend(group)
        dst[0:16, start : start + size] = src[0:16, start : start + size]
        return group

    def split(start, size):
        at = start
        while at < start + size:
            span = min(1152, start + size - at)
            yield at, span
            at += span

    def main_forward(h, start, size, n):
        base = 128 if h == 0 else 0
        for at, span in split(start, size):
            t_main[h, :, at : at + span] = mm(
                regroup, r_main[base : base + 128, at : at + span]
            ).astype(BF16)
        return plane_send(t_main.at[h], x_main.at[h], start, size, n)

    def third_forward(n):
        out_row = iota((128, 256), 0)
        column = iota((128, 256), 1)
        j = out_row >> 4
        p = (((x + (j >> 1)) & 3) << 1) | ((c + (j & 1)) & 1)
        chosen = mm(hot(column == (out_row & 15) * 16 + p), r_third[:, 0:EXT])
        spot = chosen[:, 2:3] - 1.0
        spot = (out_row & 15 == column >> 4) & (spot == (column & (spare - 1)).astype(F32))
        part_of = (column & 15) >> (spare.bit_length() - 1)
        for m in range(parts):
            match = hot(spot & (part_of == m))
            at = 2 * EXT + span3 * m
            t_third[:, at : at + span3] = mm(match, r_third[:, EXT:]).astype(BF16)
        t_third[:, 0:EXT] = mm(regroup, r_third[128:256, 0:EXT]).astype(BF16)
        t_third[:, EXT : 2 * EXT] = mm(regroup, r_third[0:128, 0:EXT]).astype(BF16)
        return plane_send(t_third, x_third, 0, 2 * EXT + width, n)

    def natural(index):
        chunk, low = index >> 7, index & 127
        j = low >> 4
        is3 = chunk == 1
        k = jnp.where(is3, low & 15, ((low >> 1) & 7) + jnp.where(chunk == 0, 8, 0))
        r = jnp.where(is3, 2, low & 1)
        source = (((x - (j >> 1)) & 3) << 1) | ((c + (j & 1)) & 1)
        return ((z + 4 + k) & 15) * 24 + source * 3 + r

    def gates_ready():
        own = pl.ds(pl.multiple_of(s * block, 128), block)
        g_all[0:ff, :] = g_ref[:, own]
        u_all[0:ff, :] = u_ref[:, own]
        order = hot(iota((block, block), 0) == natural(iota((block, block), 1)))
        for q in range(SEQ):
            if q:
                y_copies[q - 1][0].wait_recv()
                y_copies[q - 1][1].wait_recv()
            rows = slice(ff * q, ff * q + ff)
            g_perm[rows, :] = mm(g_all[rows, :], order).astype(BF16)
            u_perm[rows, :] = mm(u_all[rows, :], order).astype(BF16)

    def orders():
        restore[...] = hot(natural(iota((block, block), 0)) == iota((block, block), 1))
        row = iota((128, 128), 0)
        j = row >> 4
        target = (((x + (j >> 1)) & 3) << 1) | ((c + (j & 1)) & 1)
        for chunk in range(3):
            if chunk == 1:
                k, r = row & 15, jnp.full((128, 128), 2, jnp.int32)
            else:
                k, r = ((row >> 1) & 7) + (8 if chunk == 0 else 0), row & 1
            expert = (((z - 4 - k) & 15) << 3) | target
            first, second = ids0 == expert, ids1 == expert
            match = mm(hot(first | second), earlier) == r.astype(F32)
            owner[chunk, 0] = hot(first & match)
            owner[chunk, 1] = hot(second & match)

    def prepare(chunk):
        lanes = slice(128 * chunk, 128 * chunk + 128)
        for q in range(SEQ):
            rows = slice(ff * q, ff * q + ff)
            gate = g_perm[rows, lanes].astype(F32)
            up = u_perm[rows, lanes].astype(F32)
            sig = jax.nn.sigmoid(gate)
            activated = gate * sig
            factors[0, rows, :] = activated
            factors[1, rows, :] = activated * up
            factors[2, rows, :] = up * sig * (1.0 + gate * (1.0 - sig))

    back_copies = []
    score_copies = []

    def send_scores():
        for j in range(1, PLANE):
            copy = remote(score, score_in.at[j], ps_s.at[j], ps_r.at[j], p_from(j))
            copy.start()
            score_copies.append(copy)


    def finish(chunk, weights, cols=None):
        summed = jnp.zeros((1, 128), F32)
        for q in (2, 1, 3, 0):
            rows = slice(ff * q, ff * q + ff)
            projected = acc[rows, :]
            if cols is not None:
                projected += mm_t(
                    w_all[rows, cols[0] : cols[0] + cols[1]],
                    x_main[1, :, cols[0] : cols[0] + cols[1]],
                )
                acc[rows, :] = projected
            summed = summed + jnp.sum(factors[1, rows, :] * projected, axis=0, keepdims=True)
        score[chunk : chunk + 1, :] = summed
        if cols is not None:
            send_scores()
        for q in (2, 1, 3, 0):
            rows = slice(ff * q, ff * q + ff)
            projected = acc[rows, :]
            scaled = weights * projected
            grad_up = (scaled * factors[0, rows, :]).astype(BF16)
            grad_gate = (scaled * factors[2, rows, :]).astype(BF16)
            if q:
                grads[chunk, rows, 0:128] = grad_gate
                grads[chunk, rows, 128:256] = grad_up
                copy = remote(
                    grads.at[chunk, pl.ds(ff * q, ff)], back.at[chunk, q],
                    b_s.at[chunk, q], b_r.at[chunk, q], y_from(q),
                )
                copy.start()
                back_copies.append(copy)
            else:
                back[chunk, 0, :, 0:128] = grad_gate
                back[chunk, 0, :, 128:256] = grad_up

    def slot_weights(h):
        pick = hot(iota((16, 128), 0) == iota((16, 128), 1))
        return mm_t(pick, x_third[:, EXT * h : EXT * h + EXT])

    def spread(weights, h):
        src, dst = iota((128, 128), 0), iota((128, 128), 1)
        match = (src & 1 == 0) & (src >> 4 == dst >> 4)
        match = match & (dst & 15 == ((src >> 1) & 7) + (8 if h == 0 else 0))
        return mm(weights.astype(BF16), hot(match))

    for k in (8, 9, 15, 10, 14, 11, 13):
        whole[k].wait_recv()
    near_group = main_forward(0, 0, width, 0)
    for k in FAR[3:]:
        issue(part[k, 0])
    for k in ALL_THIRD[:9]:
        issue(third[k])
    gates_ready()
    prepare(0)
    far_groups = []

    def far_forward(n):
        for k in FAR:
            part[k, n].wait_recv()
        far_groups.append(main_forward(1, pieces[n][0], pieces[n][1], 2 + n))
        if n > 1:
            flush()

    def far_product(n):
        for copy in far_groups[n]:
            copy.wait_recv()
        start, size = pieces[n]
        return mm_t(w_all[:, start : start + size], x_main[1, :, start : start + size])

    for k in ALL_THIRD[9:]:
        issue(third[k])
    whole[0].wait_recv()
    far_forward(0)
    for k in FAR[:4]:
        issue(part[k, 1])
    orders()
    for k in ALL_THIRD:
        third[k].wait_recv()
    third_group = third_forward(1)
    for k in FAR[4:]:
        issue(part[k, 1])
    for k in FAR[:4]:
        issue(part[k, 2])
    far_forward(1)
    for k in FAR[4:]:
        issue(part[k, 2])
    for k in FAR:
        issue(part[k, 3])
    flush()
    for group in y_copies:
        group[2].wait_recv()
    for copy in near_group:
        copy.wait_recv()
    acc[...] = mm_t(w_all[...], x_main[0])
    for copy in third_group:
        copy.wait_recv()
    near_weights, far_weights = slot_weights(0), slot_weights(1)
    finish(0, near_weights[0:1, :])
    seen = jnp.maximum(x_third[:, 0:EXT].astype(F32), x_third[:, EXT : 2 * EXT].astype(F32))
    seen = jnp.max(seen, axis=0, keepdims=True)
    seen = jnp.max(jnp.where(iota((1, 128), 1) == 3, seen, 0.0), axis=1, keepdims=True)
    over[...] = jnp.broadcast_to(seen, (8, 128))
    over_copies = []
    for q in range(1, SEQ):
        copy = remote(over, over_in.at[q], o_s.at[q], o_r.at[q], y_to(q))
        copy.start()
        over_copies.append(copy)
    prepare(1)
    acc[...] = mm_t(w_all[...], x_third[:, 2 * EXT :])
    third_weights = spread(near_weights, 0) + spread(far_weights, 1)
    finish(1, third_weights[1:2, :])
    prepare(2)
    acc[...] = far_product(0)
    far_forward(2)
    acc[...] += far_product(1)

    def restored(q, chunks, first):
        value = jnp.concatenate([back[n, q, :, first : first + 128] for n in chunks], axis=1)
        return mm(value, restore[128 * chunks[0] : 128 * chunks[-1] + 128, :])

    def home(q):
        return pl.ds(pl.multiple_of(((s + q) & 3) * block, 128), block)

    far_forward(3)
    for copy in back_copies:
        copy.wait_recv()
    early = len(back_copies)
    for q in range(SEQ):
        gg_ref[:, home(q)] = restored(q, (0, 1), 0).astype(BF16)
        gu_ref[:, home(q)] = restored(q, (0, 1), 128).astype(BF16)
    acc[...] += far_product(2)
    for copy in far_groups[3]:
        copy.wait_recv()
    finish(2, far_weights[0:1, :], pieces[3])

    place = iota((8, 128), 1)
    gathered = jnp.where(place >> 4 == 0, score[...], 0.0)
    for j in range(1, PLANE):
        score_copies[j - 1].wait_recv()
        gathered = jnp.where(place >> 4 == j, score_in[j], gathered)
    total[...] = gathered
    total_copies = {}
    for k in FAR + (0, 8, 9, 15, 10, 14, 11, 13):
        copy = remote(total, total_in.at[k], zs_s.at[k], zs_r.at[k], z_from(k))
        copy.start()
        total_copies[k] = copy

    for copy in back_copies[early:]:
        copy.wait_recv()
    for q in (0, 1, 3, 2):
        for ref, first in ((gg_ref, 0), (gu_ref, 128)):
            ref[:, home(q)] = (ref[:, home(q)].astype(F32) + restored(q, (2,), first)).astype(BF16)
    worst = over[...]
    for q in range(1, SEQ):
        over_copies[q - 1].wait_recv()
        worst = jnp.maximum(worst, over_in[q])
    over_ref[0, 0] = jnp.max(worst).astype(jnp.int32)

    is3 = iota((8, 128), 0) == 1
    low = (place >> 1) & 7
    is_near = iota((8, 128), 0) == 0
    slot = jnp.where(is3, place & 15, jnp.where(is_near, low + 8, low))
    found = jnp.where(slot == SELF, total[...], 0.0)
    for k in FAR + (0, 8, 9, 15, 10, 14, 11, 13):
        total_copies[k].wait_recv()
        found = jnp.where(slot == k, total_in[k], found)
    columns = jnp.transpose(jnp.concatenate([found, jnp.zeros((120, 128), F32)], axis=0))
    result0 = jnp.zeros((1, 128), F32)
    result1 = jnp.zeros((1, 128), F32)
    for chunk in range(3):
        column = columns[:, chunk : chunk + 1]
        result0 += jnp.sum(jnp.where(owner[chunk, 0] > 0.5, column, 0.0), axis=0, keepdims=True)
        result1 += jnp.sum(jnp.where(owner[chunk, 1] > 0.5, column, 0.0), axis=0, keepdims=True)
    rg_ref[0:1, :] = result0
    rg_ref[1:2, :] = result1

    for copy in pending + plane_copies + back_copies + score_copies + over_copies:
        copy.wait_send()
    for copy in total_copies.values():
        copy.wait_send()
    for group in y_copies:
        for copy in group:
            copy.wait_send()


def exchange(spare, out_grad, expert_ids, route_weights, down_weight, gate_pre, up_pre):
    tokens, width = out_grad.shape
    ff = down_weight.shape[1]
    rows = gate_pre.shape[1]
    block = rows // SEQ
    third = width // (16 // spare)
    vmem = pl.BlockSpec(memory_space=pltpu.VMEM)
    hbm = pl.BlockSpec(memory_space=pl.ANY)
    dma = pltpu.SemaphoreType.DMA
    gate_out, up_out, route, over = pl.pallas_call(
        functools.partial(kernel, spare),
        out_shape=(
            jax.ShapeDtypeStruct((ff, rows), BF16),
            jax.ShapeDtypeStruct((ff, rows), BF16),
            jax.ShapeDtypeStruct((2, tokens), F32),
            jax.ShapeDtypeStruct((1, 1), jnp.int32),
        ),
        in_specs=[hbm, vmem, vmem, hbm, hbm, hbm],
        out_specs=(vmem, vmem, vmem, pl.BlockSpec(memory_space=pltpu.SMEM)),
        scratch_shapes=[
            pltpu.VMEM((tokens, width), BF16),
            pltpu.VMEM((ff, rows), BF16),
            pltpu.VMEM((ff, rows), BF16),
            pltpu.VMEM((256, width), BF16),
            pltpu.VMEM((256, width), BF16),
            pltpu.VMEM((256, EXT + third), BF16),
            pltpu.VMEM((256, EXT + third), BF16),
            pltpu.VMEM((2, 128, width), BF16),
            pltpu.VMEM((2, 128, width), BF16),
            pltpu.VMEM((128, 2 * EXT + width), BF16),
            pltpu.VMEM((128, 2 * EXT + width), BF16),
            pltpu.VMEM((SEQ * ff, width), BF16),
            pltpu.VMEM((SEQ * ff, block), BF16),
            pltpu.VMEM((SEQ * ff, block), BF16),
            pltpu.VMEM((SEQ * ff, block), BF16),
            pltpu.VMEM((SEQ * ff, block), BF16),
            pltpu.VMEM((3, SEQ * ff, 128), F32),
            pltpu.VMEM((block, block), BF16),
            pltpu.VMEM((3, 2, 128, tokens), BF16),
            pltpu.VMEM((SEQ * ff, 128), F32),
            pltpu.VMEM((3, SEQ * ff, 256), BF16),
            pltpu.VMEM((3, SEQ, ff, 256), BF16),
            pltpu.VMEM((8, 128), F32),
            pltpu.VMEM((PLANE, 8, 128), F32),
            pltpu.VMEM((8, 128), F32),
            pltpu.VMEM((ZN, 8, 128), F32),
            pltpu.VMEM((8, 128), F32),
            pltpu.VMEM((SEQ, 8, 128), F32),
            dma((ZN, 4)), dma((ZN, 4)), dma((ZN,)), dma((ZN,)),
            dma((6, PLANE)), dma((6, PLANE)), dma((3, SEQ)), dma((3, SEQ)),
            dma((3, SEQ)), dma((3, SEQ)), dma((PLANE,)), dma((PLANE,)),
            dma((ZN,)), dma((ZN,)), dma((SEQ,)), dma((SEQ,)), dma((4,)),
        ],
        compiler_params=pltpu.CompilerParams(
            collective_id=0 if spare == 4 else 1, has_side_effects=True, vmem_limit_bytes=56 * 2**20
        ),
        cost_estimate=pl.CostEstimate(
            flops=2 * SEQ * ff * width * block, bytes_accessed=8 * 2**20, transcendentals=0
        ),
        name="expert_backward_%d" % spare,
    )(
        out_grad,
        expert_ids.T,
        route_weights.T,
        down_weight[0],
        gate_pre[0].T,
        up_pre[0].T,
    )
    return gate_out, up_out, route, over


def per_device(*arrays):
    gate_out, up_out, route, over = exchange(4, *arrays)
    gate_out, up_out, route = lax.cond(
        over[0, 0] > 0,
        lambda: exchange(8, *arrays)[:3],
        lambda: (gate_out, up_out, route),
    )
    return gate_out.T[None], up_out.T[None], route.T


def solution(mesh):
    placed = (
        P(("seq", "exp"), None),
        P(("seq", "exp"), None),
        P(("seq", "exp"), None),
        P("exp", "seq", None),
        P("exp", None, "seq"),
        P("exp", None, "seq"),
    )
    return jax.shard_map(
        per_device,
        mesh=mesh,
        in_specs=placed,
        out_specs=(P("exp", None, "seq"), P("exp", None, "seq"), P(("seq", "exp"), None)),
        check_vma=False,
    )
```
